768 devices in a mesh: dom: 12 (over z), grp: 64 (over x, y, core).
Axes of the slice: x: 4, y: 8, z: 12, core: 2. Of those that a mesh axis runs over, the one named last changes fastest.
Arguments:
- a_blocks: bfloat16 [18432, 7, 4096], P(('dom', 'grp')), may hold values from -0.75 to 0.75
- p_blocks: bfloat16 [18432, 4096], P(('dom', 'grp')), may hold values from -1.1953125 to 1.1953125
- columns: int32 [18432, 7], P(('dom', 'grp')), may hold values from 0 to 18431, as said below
- targets: int32 [18432, 7], P(('dom', 'grp')), may hold values from 0 to 24575, as said below
Outputs:
- coarse: float32 [24576, 4096], P(('dom', 'grp'))
The draws below stay inside these ranges and needn't reach their ends.
Inputs may be any that keep to these rules, and one draw needn't show every extreme that they name: `columns`: slot 0 of element e is e itself. Every other entry of an element held by device index r (elements r * 24 to (r + 1) * 24 - 1, devices in dom-major order) names an element of device r, one of the last 6 elements of device r - 64, or one of the first 6 elements of device r + 64, the latter two only where that device exists. `targets`: A target of an element of device r names a coarse block of device r or of another device with the same dom index (blocks q * 32 to (q + 1) * 32 - 1 belong to device q). Of the entries of one device, at most 2 name blocks of any one other device; for each dom index some device receives exactly 2 from every other device of that dom index.
All inputs are finite; a program needn't handle non-finite values.
Results may differ from the reference program's by a relative error of at most 0.0029.
Values may be sent and summed in bfloat16 or wider, within the bound.
A program may use at most 64 MiB of HBM per device.

```python
import jax
import jax.numpy as jnp
from jax import lax

BS = 64
K = 7
E_DEV = 24
HALO = 6
CAP = 2
CB_DEV = 32
ELEMS = 18432
CBLOCKS = 24576
N_DOM = 12
N_GRP = 64


def draw_columns(key, part):
    key = jax.random.fold_in(key, 11)
    total = E_DEV * N_DOM * N_GRP
    element = jnp.arange(total, dtype=jnp.int32)
    device = element // E_DEV
    row = device // N_GRP
    key_kind, key_local, key_lower, key_upper = jax.random.split(key, 4)
    kind = jax.random.randint(key_kind, (total, K), 0, 4)
    kind = jnp.where((kind == 2) & (row[:, None] == 0), 0, kind)
    kind = jnp.where((kind == 3) & (row[:, None] == N_DOM - 1), 1, kind)
    local = device[:, None] * E_DEV + jax.random.randint(key_local, (total, K), 0, E_DEV)
    lower = (device[:, None] - N_GRP) * E_DEV + E_DEV - HALO + jax.random.randint(key_lower, (total, K), 0, HALO)
    upper = (device[:, None] + N_GRP) * E_DEV + jax.random.randint(key_upper, (total, K), 0, HALO)
    picked = jnp.where(kind == 2, lower, jnp.where(kind == 3, upper, local))
    picked = picked.at[:, 0].set(element)
    return picked.astype(jnp.int32)


def draw_targets(key, part):
    key = jax.random.fold_in(key, 23)
    key_hot, key_count, key_order, key_block = jax.random.split(key, 4)
    devices = N_DOM * N_GRP
    units = E_DEV * K
    device = jnp.arange(devices, dtype=jnp.int32)
    row = device // N_GRP
    self_peer = device % N_GRP
    hot = jax.random.randint(key_hot, (N_DOM,), 0, N_GRP)
    counts = jax.random.randint(key_count, (devices, N_GRP), 0, CAP + 1)
    peers = jnp.arange(N_GRP, dtype=jnp.int32)
    counts = jnp.where(peers[None, :] == hot[row][:, None], CAP, counts)
    counts = jnp.where(peers[None, :] == self_peer[:, None], 0, counts)
    ends = jnp.cumsum(counts, axis=1)
    position = jnp.arange(units, dtype=jnp.int32)
    dest = jnp.sum((ends[:, None, :] <= position[None, :, None]).astype(jnp.int32), axis=2)
    order_keys = jax.random.split(key_order, devices)
    order = jax.vmap(lambda one: jax.random.permutation(one, units))(order_keys)
    dest = jnp.take_along_axis(dest, order, axis=1)
    peer = jnp.where(dest == N_GRP, self_peer[:, None], dest)
    block = jax.random.randint(key_block, (devices, units), 0, CB_DEV)
    chosen = (row[:, None] * N_GRP + peer) * CB_DEV + block
    return chosen.reshape(devices * E_DEV, K).astype(jnp.int32)


def steps_of(rng, dims, cuts, low, top_value):
    factor_of = 1.0
    for dim, parts in cuts:
        heights = jax.random.uniform(jax.random.fold_in(jax.random.fold_in(rng, 6), dim), (parts,), jnp.float32, low / len(cuts), top_value / len(cuts))
        factor_of = factor_of * jnp.repeat(jnp.exp(heights), dims[dim] // parts).reshape((-1,) + (1,) * (len(dims) - 1 - dim))
    return factor_of


def scatter_about(key, shape, spread, limit, cuts=(), kind=jnp.bfloat16):
    values = spread * jax.random.normal(key, shape, jnp.float32)
    if cuts:
        values = values * steps_of(key, shape, cuts, -0.22, 0.18)
    return jnp.clip(values, -limit, limit).astype(kind)


def setup_inputs(seed: int = 0) -> dict:
    key_list = jax.random.split(jax.random.key(seed), 5)
    a_blocks = scatter_about(key_list[0], (ELEMS, K, BS * BS), BS ** -0.5, 0.75, ((0, 768),))
    p_blocks = scatter_about(key_list[1], (ELEMS, BS * BS), 0.2, 1.1953125, ((0, 768),))
    columns = draw_columns(jax.random.fold_in(key_list[4], 71), 0)
    targets = draw_targets(jax.random.fold_in(key_list[4], 71), 0)
    return {"a_blocks": a_blocks, "p_blocks": p_blocks, "columns": columns, "targets": targets}


def reference(a_blocks, p_blocks, columns, targets):
    span = N_GRP * E_DEV
    row_blocks = N_GRP * CB_DEV

    def one_row(row):
        start = (row * span).astype(jnp.int32)
        a_part = lax.dynamic_slice_in_dim(a_blocks, start, span, 0).astype(jnp.float32).reshape(span, K, BS, BS)
        col_part = lax.dynamic_slice_in_dim(columns, start, span, 0)
        tgt_part = lax.dynamic_slice_in_dim(targets, start, span, 0)
        own = lax.dynamic_slice_in_dim(p_blocks, start, span, 0).astype(jnp.float32).reshape(span, BS, BS)
        neighbours = jnp.take(p_blocks, col_part.reshape(-1), axis=0).astype(jnp.float32).reshape(span, K, BS, BS)
        product = jnp.einsum("ekij,ekjl->ekil", a_part, neighbours, precision=lax.Precision.HIGHEST)
        product = lax.optimization_barrier(product.astype(jnp.bfloat16)).astype(jnp.float32)
        terms = jnp.einsum("eji,ekjl->ekil", own, product, precision=lax.Precision.HIGHEST).reshape(span * K, BS * BS)
        local_slot = (tgt_part.reshape(-1) - row * row_blocks).astype(jnp.int32)
        return jax.ops.segment_sum(terms, local_slot, num_segments=row_blocks)

    result = lax.map(one_row, jnp.arange(N_DOM, dtype=jnp.int32))
    return result.reshape(CBLOCKS, BS * BS)
```

```python
import functools

import jax
import jax.numpy as jnp
from jax import lax
from jax.experimental import pallas as pl
from jax.experimental.pallas import tpu as pltpu
from jax.sharding import PartitionSpec as P

MESH = pl.DeviceIdType.MESH
F32 = jnp.float32
BF16 = jnp.bfloat16
I32 = jnp.int32

E = 24
K = 7
HALO = 6
CB = 32
CAP = 2
NG = 64
R = 32
L = 128
UNITS = E * K
NP = E + 2 * HALO


def iota(shape, dim):
    return lax.broadcasted_iota(I32, shape, dim)


def split(u):
    k = (u * 2731) >> 16
    return k, u - k * E


def peer_of(me, d):
    return lax.rem(me + d, NG)


def routing(tgt_v, device):
    t = tgt_v[...]
    owner = t >> 5
    col = t & (CB - 1)
    home = owner == device
    dest = jnp.where(home, NG, owner & (NG - 1)).astype(F32)
    key = jnp.where(home, col, CB).astype(F32)
    colf = col.astype(F32)
    unit_k, unit_e = split(iota((UNITS, K), 0)), split(iota((UNITS, E), 0))
    spread = jnp.where(unit_k[0] == iota((UNITS, K), 1), 1.0, 0.0).astype(F32)
    mine = unit_e[1] == iota((UNITS, E), 1)

    def column(x):
        wide = jnp.dot(spread, x, preferred_element_type=F32)
        return jnp.sum(jnp.where(mine, wide, 0.0), axis=1, keepdims=True)

    dest_c = column(dest)
    key_c = column(key)
    col_c = column(colf)
    pick = jnp.where(split(iota((E, UNITS), 1))[1] == iota((E, UNITS), 0), 1.0, 0.0).astype(F32)
    wide = jnp.dot(key, pick, preferred_element_type=F32)
    mine_r = split(iota((K, UNITS), 1))[0] == iota((K, UNITS), 0)
    key_r = jnp.sum(jnp.where(mine_r, wide, 0.0), axis=0, keepdims=True)
    unit_c = iota((UNITS, 1), 0).astype(F32)
    chosen = dest_c == iota((UNITS, L), 1).astype(F32)
    chosen = jnp.where(iota((UNITS, L), 1) < NG, jnp.where(chosen, 1.0, 0.0), 0.0)
    before = jnp.where(iota((UNITS, UNITS), 1) < iota((UNITS, UNITS), 0), 1.0, 0.0)
    rank = jnp.dot(before.astype(BF16), chosen.astype(BF16), preferred_element_type=F32)
    first = jnp.where(rank == 0.0, chosen, 0.0)
    second = jnp.where(rank == 1.0, chosen, 0.0)

    def row(x):
        return jnp.sum(x, axis=0, keepdims=True)

    rows = [
        row(first * unit_c),
        row(second * unit_c),
        row(first * (col_c - CB)) + CB,
        row(second * (col_c - CB)) + CB,
    ]
    full_c = key_c * 256.0 + unit_c
    full_r = key_r * 256.0 + iota((1, UNITS), 1).astype(F32)
    rank_c = jnp.sum(jnp.where(full_r < full_c, 1.0, 0.0), axis=1, keepdims=True)
    at = jnp.where(rank_c == iota((UNITS, 2 * L), 1).astype(F32), 1.0, 0.0)
    perm = row(at * unit_c)
    skey = row(at * key_c)
    slot = iota((UNITS, L), 1).astype(F32)
    upto = row(jnp.where(key_c <= slot, 1.0, 0.0))
    count = row(jnp.where(key_c == slot, 1.0, 0.0))
    rows += [perm[:, :L], perm[:, L:], skey[:, :L], skey[:, L:], jnp.maximum(upto - 1.0, 0.0), jnp.minimum(count, 1.0)]
    rows += [jnp.zeros((1, L), F32)] * (16 - len(rows))
    return jnp.concatenate(rows, axis=0).astype(I32)


def exchange(a_ref, p_ref, col_ref, tgt_ref, recv_ref, lab_ref, home_ref,
             a_v, p_v, col_s, tgt_v, tab_v, tab_s, pf, p2, std_a, std_b, w, ptx, af, a2,
             send_v, lab_v, acc_v, home_v,
             a_sem, p_sem, small_sem, halo_send, halo_recv, pay_send, pay_recv, lab_send, lab_recv):
    dom, me = lax.axis_index("dom"), lax.axis_index("grp")
    doms = lax.axis_size("dom")
    device = dom * NG + me
    has_low = dom > 0
    has_high = dom < doms - 1

    barrier = pltpu.get_barrier_semaphore()

    @pl.when(has_low)
    def _():
        pl.semaphore_signal(barrier, inc=1, device_id=(dom - 1, me), device_id_type=MESH)

    @pl.when(has_high)
    def _():
        pl.semaphore_signal(barrier, inc=1, device_id=(dom + 1, me), device_id_type=MESH)

    def greet(d, c):
        pl.semaphore_signal(barrier, inc=1, device_id=(dom, peer_of(me, d)), device_id_type=MESH)
        return c

    lax.fori_loop(1, NG, greet, 0)

    p_copy = pltpu.make_async_copy(p_ref, p_v, p_sem)
    p_copy.start()
    tgt_copy = pltpu.make_async_copy(tgt_ref, tgt_v, small_sem.at[0])
    tgt_copy.start()
    col_copy = pltpu.make_async_copy(col_ref, col_s, small_sem.at[1])
    col_copy.start()
    a_copies = [
        pltpu.make_async_copy(a_ref.at[i], a_v.at[i], a_sem.at[i]) for i in range(K)
    ]
    for c in a_copies:
        c.start()

    p_copy.wait()
    for r in range(R):
        pf[pl.ds(r * E, E), :] = p_v[:, r * L:(r + 1) * L].astype(F32)

    def own(e, c):
        p2[HALO + e] = pf[pl.ds(e, R, stride=E), :].astype(BF16)
        return c

    lax.fori_loop(0, E, own, 0, unroll=4)

    @pl.when(jnp.logical_not(has_low))
    def _():
        p2[pl.ds(0, HALO)] = jnp.zeros((HALO, R, L), BF16)

    @pl.when(jnp.logical_not(has_high))
    def _():
        p2[pl.ds(HALO + E, HALO)] = jnp.zeros((HALO, R, L), BF16)

    left = iota((64, L), 1) < 64
    left32 = iota((R, L), 1) < 64

    def spread_block(c, x):
        xr = pltpu.roll(x, 64, 1)
        std_a[pl.ds(0, R, stride=2), :] = x
        std_a[pl.ds(1, R, stride=2), :] = xr
        std_b[pl.ds(0, R, stride=2), :] = xr
        std_b[pl.ds(1, R, stride=2), :] = x
        lo = jnp.where(left, std_a[0:64, :], 0.0).astype(BF16)
        hi = jnp.where(left, 0.0, std_b[0:64, :]).astype(BF16)
        w[c, 0:64, 0:L] = lo
        w[c, 0:64, L:2 * L] = hi
        w[c, 64:128, 0:L] = hi
        w[c, 64:128, L:2 * L] = lo

    pl.semaphore_wait(barrier, NG - 1 + has_low.astype(I32) + has_high.astype(I32))

    def halo(up):
        src = p2.at[pl.ds(E, HALO)] if up else p2.at[pl.ds(HALO, HALO)]
        dst = p2.at[pl.ds(0, HALO)] if up else p2.at[pl.ds(HALO + E, HALO)]
        i = 0 if up else 1
        return pltpu.make_async_remote_copy(
            src_ref=src, dst_ref=dst, send_sem=halo_send.at[i], recv_sem=halo_recv.at[i],
            device_id=(dom + 1 if up else dom - 1, me), device_id_type=MESH)

    @pl.when(has_high)
    def _():
        halo(True).start()

    @pl.when(has_low)
    def _():
        halo(False).start()

    tgt_copy.wait()
    tab_v[...] = routing(tgt_v, device)
    tab_copy = pltpu.make_async_copy(tab_v, tab_s, small_sem.at[2])
    tab_copy.start()

    to = iota((L, L), 1)
    moved = jnp.where(iota((L, L), 0) == (to & 64) + ((to & 31) << 1) + ((to >> 5) & 1), 1.0, 0.0).astype(BF16)

    def prepare(e, c):
        x = pf[pl.ds(e, R, stride=E), :]
        spread_block(HALO + e, x)
        x = jnp.dot(x.astype(BF16), moved, preferred_element_type=F32)
        stacked = jnp.concatenate(
            [x, pltpu.roll(x, 32, 1), pltpu.roll(x, 64, 1), pltpu.roll(x, 96, 1)], axis=0)
        ptx[e] = stacked.T[0:R, :].astype(BF16)
        return c

    lax.fori_loop(0, E, prepare, 0)

    def unpack(k, c):
        for r in range(R):
            af[pl.ds(r * E, E), :] = a_v[k, :, r * L:(r + 1) * L].astype(F32)
        for e in range(E):
            a2[k * E + e] = af[pl.ds(e, R, stride=E), :].astype(BF16)
        return c

    for i in range(K):
        a_copies[i].wait()
    lax.fori_loop(0, K, unpack, 0)
    col_copy.wait()
    tab_copy.wait()

    @pl.when(has_low)
    def _():
        halo(True).wait_recv()

    @pl.when(has_high)
    def _():
        halo(False).wait_recv()

    def prepare_halo(i, c):
        at = jnp.where(i < HALO, i, i + E)
        spread_block(at, p2[at].astype(F32))
        return c

    lax.fori_loop(0, 2 * HALO, prepare_halo, 0)

    first_own = device * E

    def term(u):
        u = jnp.clip(u, 0, UNITS - 1)
        k, e = split(u)
        rel = col_s[k, e] - first_own
        at = jnp.where(rel < 0, rel + NG * E - (E - HALO), jnp.where(rel < E, rel + HALO, rel - NG * E + HALO + E))
        at = jnp.clip(at, 0, NP - 1)
        out = jnp.dot(a2[u], w[at], preferred_element_type=F32)
        one, two = out[:, :L], out[:, L:]
        right = jnp.concatenate(
            [jnp.where(left32, one, 0.0), jnp.where(left32, 0.0, one),
             jnp.where(left32, two, 0.0), jnp.where(left32, 0.0, two)], axis=0).astype(BF16)
        return jnp.dot(ptx[e], right, preferred_element_type=F32)

    def pay(d):
        return pltpu.make_async_remote_copy(
            src_ref=send_v.at[d], dst_ref=recv_ref.at[d], send_sem=pay_send, recv_sem=pay_recv,
            device_id=(dom, peer_of(me, d)), device_id_type=MESH)

    def lab(d):
        return pltpu.make_async_remote_copy(
            src_ref=lab_v.at[d], dst_ref=lab_ref.at[d], send_sem=lab_send, recv_sem=lab_recv,
            device_id=(dom, peer_of(me, d)), device_id_type=MESH)

    lane = iota((1, L), 1)
    group = 3

    def send(i, c):
        for j in range(group):
            d = 1 + i * group + j
            q = peer_of(me, d)
            for s in range(CAP):
                send_v[d, s * R:(s + 1) * R, :] = term(tab_s[s, q]).astype(BF16)
            lab_v[d] = jnp.where(lane == 0, tab_s[2, q], tab_s[3, q])
        for j in range(group):
            d = 1 + i * group + j
            pay(d).start()
            lab(d).start()
        return c

    lax.fori_loop(0, (NG - 1) // group, send, 0)

    def at_home(i, acc):
        n = i * 4
        terms = []
        for j in range(4):
            pos = n + j
            terms.append(term(tab_s[4 + pos // L, lax.rem(pos, L)]))
        for j in range(4):
            pos = n + j
            prev = jnp.maximum(pos - 1, 0)
            same = (tab_s[6 + pos // L, lax.rem(pos, L)] == tab_s[6 + prev // L, lax.rem(prev, L)]).astype(F32)
            acc = acc * same + terms[j]
            acc_v[pos] = acc
        return acc

    lax.fori_loop(0, E * K // 4, at_home, jnp.zeros((R, L), F32))

    def fetch(t, c):
        home_v[t] = acc_v[jnp.clip(tab_s[8, t], 0, UNITS - 1)] * tab_s[9, t].astype(F32)
        return c

    lax.fori_loop(0, CB, fetch, 0, unroll=4)
    home_copy = pltpu.make_async_copy(home_v, home_ref, small_sem.at[3])
    home_copy.start()

    def all_pay():
        return pltpu.make_async_remote_copy(
            src_ref=send_v.at[pl.ds(1, NG - 1)], dst_ref=recv_ref.at[pl.ds(1, NG - 1)], send_sem=pay_send,
            recv_sem=pay_recv, device_id=(dom, peer_of(me, 1)), device_id_type=MESH)

    def all_lab():
        return pltpu.make_async_remote_copy(
            src_ref=lab_v.at[pl.ds(1, NG - 1)], dst_ref=lab_ref.at[pl.ds(1, NG - 1)], send_sem=lab_send,
            recv_sem=lab_recv, device_id=(dom, peer_of(me, 1)), device_id_type=MESH)

    @pl.when(has_high)
    def _():
        halo(True).wait_send()

    @pl.when(has_low)
    def _():
        halo(False).wait_send()

    home_copy.wait()
    all_lab().wait()
    all_pay().wait()


def collect(recv_ref, lab_ref, home_ref, out_ref, recv_v, lab_s, acc, turned, rsem, lsem, hsem):
    lab_copy = pltpu.make_async_copy(lab_ref, lab_s, lsem)
    lab_copy.start()
    home_copy = pltpu.make_async_copy(home_ref, acc.at[pl.ds(0, CB)], hsem)
    home_copy.start()
    copies = [pltpu.make_async_copy(recv_ref.at[pl.ds(i * 8, 8)], recv_v.at[pl.ds(i * 8, 8)], rsem.at[i]) for i in range(8)]
    for c in copies:
        c.start()
    lab_copy.wait()
    home_copy.wait()

    def add(d, c):
        for s in range(CAP):
            t = jnp.clip(lab_s[d, 0, s], 0, CB)
            acc[t] = acc[t] + recv_v[d, s * R:(s + 1) * R, :].astype(F32)
        return c

    for i in range(8):
        copies[i].wait()
        lax.fori_loop(max(1, i * 8), i * 8 + 8, add, 0)

    def turn(t, c):
        turned[pl.ds(t, R, stride=CB), :] = acc[t]
        return c

    lax.fori_loop(0, CB, turn, 0, unroll=4)
    for r in range(R):
        out_ref[:, r * L:(r + 1) * L] = turned[r * CB:(r + 1) * CB, :]


def on_device(a_blocks, p_blocks, columns, targets):
    hbm = pl.BlockSpec(memory_space=pl.ANY)
    dma = pltpu.SemaphoreType.DMA
    recv, labels, home = pl.pallas_call(
        exchange,
        out_shape=(
            jax.ShapeDtypeStruct((NG, CAP * R, L), BF16),
            jax.ShapeDtypeStruct((NG, 1, L), I32),
            jax.ShapeDtypeStruct((CB, R, L), F32),
        ),
        in_specs=[hbm] * 4,
        out_specs=(hbm, hbm, hbm),
        scratch_shapes=[
            pltpu.VMEM((K, E, 64 * 64), BF16),
            pltpu.VMEM((E, 64 * 64), BF16),
            pltpu.SMEM((K, E), I32),
            pltpu.VMEM((K, E), I32),
            pltpu.VMEM((16, L), I32),
            pltpu.SMEM((16, L), I32),
            pltpu.VMEM((R * E + E, L), F32),
            pltpu.VMEM((NP, R, L), BF16),
            pltpu.VMEM((72, L), F32),
            pltpu.VMEM((72, L), F32),
            pltpu.VMEM((NP, L, 2 * L), BF16),
            pltpu.VMEM((E, R, L), BF16),
            pltpu.VMEM((R * E + E, L), F32),
            pltpu.VMEM((UNITS, R, L), BF16),
            pltpu.VMEM((NG, CAP * R, L), BF16),
            pltpu.VMEM((NG, 1, L), I32),
            pltpu.VMEM((E * K, R, L), F32),
            pltpu.VMEM((CB, R, L), F32),
            dma((K,)), dma, dma((4,)), dma((2,)), dma((2,)), dma, dma, dma, dma,
        ],
        compiler_params=pltpu.CompilerParams(
            collective_id=0, has_side_effects=True, vmem_limit_bytes=62 * 1024 * 1024),
    )(a_blocks.transpose(1, 0, 2), p_blocks, columns.T, targets.T)
    return pl.pallas_call(
        collect,
        out_shape=jax.ShapeDtypeStruct((CB, 64 * 64), F32),
        in_specs=[hbm] * 3,
        out_specs=pl.BlockSpec(memory_space=pltpu.VMEM),
        scratch_shapes=[
            pltpu.VMEM((NG, CAP * R, L), BF16),
            pltpu.SMEM((NG, 1, L), I32),
            pltpu.VMEM((CB + 1, R, L), F32),
            pltpu.VMEM((R * CB + CB, L), F32),
            dma((8,)), dma, dma,
        ],
        compiler_params=pltpu.CompilerParams(vmem_limit_bytes=62 * 1024 * 1024),
    )(recv, labels, home)


def solution(mesh):
    spec = P(("dom", "grp"), None)
    return jax.shard_map(
        on_device, mesh=mesh, in_specs=(P(("dom", "grp"), None, None), spec, spec, spec), out_specs=spec,
        check_vma=False)
```

```python
import functools

import jax
import jax.numpy as jnp
from jax import lax
from jax.experimental import pallas as pl
from jax.experimental.pallas import tpu as pltpu
from jax.sharding import PartitionSpec as P

MESH = pl.DeviceIdType.MESH
F32 = jnp.float32
BF16 = jnp.bfloat16
I32 = jnp.int32

E = 24
K = 7
HALO = 6
CB = 32
CAP = 2
NG = 64
R = 32
L = 128
UNITS = E * K
NP = E + 2 * HALO


def iota(shape, dim):
    return lax.broadcasted_iota(I32, shape, dim)


def split(u):
    k = (u * 2731) >> 16
    return k, u - k * E


def kind_of(dom, g):
    return jnp.where((dom == 0) & (g == 0), 2, jnp.where(((g >> 1) & 7) == 4, 1, 0))


def routing(tgt_v, device):
    t = tgt_v[...]
    owner = t >> 5
    col = t & (CB - 1)
    home = owner == device
    dest = jnp.where(home, NG, owner & (NG - 1)).astype(F32)
    key = jnp.where(home, col, CB).astype(F32)
    colf = col.astype(F32)
    unit_k, unit_e = split(iota((UNITS, K), 0)), split(iota((UNITS, E), 0))
    spread = jnp.where(unit_k[0] == iota((UNITS, K), 1), 1.0, 0.0).astype(F32)
    mine = unit_e[1] == iota((UNITS, E), 1)

    def column(x):
        wide = jnp.dot(spread, x, preferred_element_type=F32)
        return jnp.sum(jnp.where(mine, wide, 0.0), axis=1, keepdims=True)

    dest_c = column(dest)
    key_c = column(key)
    col_c = column(colf)
    pick = jnp.where(split(iota((E, UNITS), 1))[1] == iota((E, UNITS), 0), 1.0, 0.0).astype(F32)
    wide = jnp.dot(key, pick, preferred_element_type=F32)
    mine_r = split(iota((K, UNITS), 1))[0] == iota((K, UNITS), 0)
    key_r = jnp.sum(jnp.where(mine_r, wide, 0.0), axis=0, keepdims=True)
    unit_c = iota((UNITS, 1), 0).astype(F32)
    chosen = dest_c == iota((UNITS, L), 1).astype(F32)
    chosen = jnp.where(iota((UNITS, L), 1) < NG, jnp.where(chosen, 1.0, 0.0), 0.0)
    before = jnp.where(iota((UNITS, UNITS), 1) < iota((UNITS, UNITS), 0), 1.0, 0.0)
    rank = jnp.dot(before.astype(BF16), chosen.astype(BF16), preferred_element_type=F32)
    first = jnp.where(rank == 0.0, chosen, 0.0)
    second = jnp.where(rank == 1.0, chosen, 0.0)

    def row(x):
        return jnp.sum(x, axis=0, keepdims=True)

    rows = [
        row(first * unit_c),
        row(second * unit_c),
        row(first * (col_c - CB)) + CB,
        row(second * (col_c - CB)) + CB,
    ]
    full_c = key_c * 256.0 + unit_c
    full_r = key_r * 256.0 + iota((1, UNITS), 1).astype(F32)
    rank_c = jnp.sum(jnp.where(full_r < full_c, 1.0, 0.0), axis=1, keepdims=True)
    at = jnp.where(rank_c == iota((UNITS, 2 * L), 1).astype(F32), 1.0, 0.0)
    perm = row(at * unit_c)
    skey = row(at * key_c)
    slot = iota((UNITS, L), 1).astype(F32)
    upto = row(jnp.where(key_c <= slot, 1.0, 0.0))
    count = row(jnp.where(key_c == slot, 1.0, 0.0))
    rows += [perm[:, :L], perm[:, L:], skey[:, :L], skey[:, L:], jnp.maximum(upto - 1.0, 0.0), jnp.minimum(count, 1.0)]
    rows += [jnp.zeros((1, L), F32)] * (16 - len(rows))
    return jnp.concatenate(rows, axis=0).astype(I32)


def exchange(a_ref, p_ref, col_ref, tgt_ref, recv_ref, lab_ref, home_ref,
             a_v, p_v, col_s, tgt_v, tab_v, tab_s, pf, p2, w, ptx, af, a2,
             send_v, lab_v, acc_v, home_v,
             a_sem, p_sem, small_sem, halo_send, halo_recv, pay_send, pay_recv, lab_send, lab_recv, late, late_z):
    dom, me = lax.axis_index("dom"), lax.axis_index("grp")
    doms = lax.axis_size("dom")
    device = dom * NG + me
    x, y, core = me >> 4, (me >> 1) & 7, me & 1
    kind = kind_of(dom, me)
    has_low = dom > 0
    has_high = dom < doms - 1
    above_first = (dom == 1) & (me == 0)

    p_copy = pltpu.make_async_copy(p_ref, p_v, p_sem)
    p_copy.start()

    barrier = pltpu.get_barrier_semaphore()

    @pl.when(has_low)
    def _():
        pl.semaphore_signal(barrier, inc=1, device_id=(dom - 1, me), device_id_type=MESH)

    @pl.when(has_high & (kind < 2))
    def _():
        pl.semaphore_signal(barrier, inc=1, device_id=(dom + 1, me), device_id_type=MESH)

    def greet(d, c):
        q = (me + d) & (NG - 1)

        @pl.when(kind <= kind_of(dom, q))
        def _():
            pl.semaphore_signal(barrier, inc=1, device_id=(dom, q), device_id_type=MESH)

        return c

    lax.fori_loop(1, NG, greet, 0)

    tgt_copy = pltpu.make_async_copy(tgt_ref, tgt_v, small_sem.at[0])
    tgt_copy.start()
    col_copy = pltpu.make_async_copy(col_ref, col_s, small_sem.at[1])
    col_copy.start()
    a_copies = [pltpu.make_async_copy(a_ref.at[i], a_v.at[i], a_sem.at[i]) for i in range(K)]
    for c in a_copies:
        c.start()

    p_copy.wait()
    for r in range(R):
        pf[pl.ds(r * E, E), :] = p_v[:, r * L:(r + 1) * L].astype(F32)

    def own(e, c):
        p2[HALO + e] = pf[pl.ds(e, R, stride=E), :].astype(BF16)
        return c

    lax.fori_loop(0, E, own, 0, unroll=8)

    @pl.when(jnp.logical_not(has_low))
    def _():
        p2[pl.ds(0, HALO)] = jnp.zeros((HALO, R, L), BF16)

    @pl.when(jnp.logical_not(has_high))
    def _():
        p2[pl.ds(HALO + E, HALO)] = jnp.zeros((HALO, R, L), BF16)

    def halo(up):
        src = p2.at[pl.ds(E, HALO)] if up else p2.at[pl.ds(HALO, HALO)]
        dst = p2.at[pl.ds(0, HALO)] if up else p2.at[pl.ds(HALO + E, HALO)]
        i = 0 if up else 1
        return pltpu.make_async_remote_copy(
            src_ref=src, dst_ref=dst, send_sem=halo_send.at[i], recv_sem=halo_recv.at[i],
            device_id=(dom + 1 if up else dom - 1, me), device_id_type=MESH)

    def met():
        early = 7 * 8 - (dom == 0).astype(I32)
        peers = jnp.where(kind == 0, early - 1, jnp.where(kind == 1, early + 8 - 1, NG - 1))
        low = (has_low & jnp.logical_not(above_first)).astype(I32)
        pl.semaphore_wait(barrier, peers + low + has_high.astype(I32))

    def send_halo():
        @pl.when(has_high)
        def _():
            halo(True).start()

        @pl.when(above_first)
        def _():
            pl.semaphore_wait(late_z, 1)

        @pl.when(has_low)
        def _():
            halo(False).start()

    @pl.when(kind > 0)
    def _():
        met()

        @pl.when(kind == 2)
        def _():
            pl.semaphore_signal(late_z, inc=1, device_id=(dom + 1, me), device_id_type=MESH)

        send_halo()

        def answer(d, c):
            q = (me + d) & (NG - 1)

            @pl.when(kind_of(dom, q) < kind)
            def _():
                pl.semaphore_signal(late.at[kind - 1], inc=1, device_id=(dom, q), device_id_type=MESH)

            return c

        lax.fori_loop(1, NG, answer, 0)

    tgt_copy.wait()
    tab_v[...] = routing(tgt_v, device)
    tab_copy = pltpu.make_async_copy(tab_v, tab_s, small_sem.at[2])
    tab_copy.start()

    left = iota((R, L), 1) < 64
    row64, col64 = iota((64, 64), 0), iota((64, 64), 1)
    woven = jnp.where(row64 == ((col64 & 31) << 1) + (col64 >> 5), 1.0, 0.0).astype(BF16)
    even = jnp.where(iota((R, L), 1) == iota((R, L), 0) * 2, 1.0, 0.0).astype(BF16)

    def spread_block(c, b):
        br = pltpu.roll(b, 64, 1)
        parts = jnp.concatenate(
            [jnp.concatenate([jnp.where(left, b, 0.0), jnp.where(left, 0.0, br)], axis=1),
             jnp.concatenate([jnp.where(left, br, 0.0), jnp.where(left, 0.0, b)], axis=1)], axis=0).astype(BF16)
        z = jnp.dot(woven, parts, preferred_element_type=F32).astype(BF16)
        w[c, 0:64, :] = z
        w[c, 64:128, 0:L] = z[:, L:]
        w[c, 64:128, L:2 * L] = z[:, :L]

    def prepare(e, c):
        b = pf[pl.ds(e, R, stride=E), :]
        spread_block(HALO + e, b)
        stacked = jnp.concatenate(
            [b, pltpu.roll(b, 63, 1), pltpu.roll(b, 64, 1), pltpu.roll(b, 127, 1)], axis=0).astype(BF16)
        ptx[e] = lax.dot_general(
            even, stacked, (((1,), (1,)), ((), ())), preferred_element_type=F32).astype(BF16)
        return c

    lax.fori_loop(0, E, prepare, 0, unroll=4)

    def unpack(k, c):
        for r in range(R):
            af[pl.ds(r * E, E), :] = a_v[k, :, r * L:(r + 1) * L].astype(F32)
        for e in range(E):
            a2[k * E + e] = af[pl.ds(e, R, stride=E), :].astype(BF16)
        return c

    for i in range(K):
        a_copies[i].wait()
    lax.fori_loop(0, K, unpack, 0)
    col_copy.wait()
    tab_copy.wait()

    @pl.when(kind == 0)
    def _():
        met()
        send_halo()

    @pl.when(has_low)
    def _():
        halo(True).wait_recv()

    @pl.when(has_high)
    def _():
        halo(False).wait_recv()

    def prepare_halo(i, c):
        at = jnp.where(i < HALO, i, i + E)
        spread_block(at, p2[at].astype(F32))
        return c

    lax.fori_loop(0, 2 * HALO, prepare_halo, 0, unroll=4)

    first_own = device * E

    def term(u):
        u = jnp.clip(u, 0, UNITS - 1)
        k, e = split(u)
        rel = col_s[k, e] - first_own
        at = jnp.where(rel < 0, rel + NG * E - (E - HALO), jnp.where(rel < E, rel + HALO, rel - NG * E + HALO + E))
        at = jnp.clip(at, 0, NP - 1)
        out = jnp.dot(a2[u], w[at], preferred_element_type=F32)
        one, two = out[:, :L], out[:, L:]
        right = jnp.concatenate(
            [jnp.where(left, one, 0.0), jnp.where(left, 0.0, one),
             jnp.where(left, two, 0.0), jnp.where(left, 0.0, two)], axis=0).astype(BF16)
        return jnp.dot(ptx[e], right, preferred_element_type=F32)

    def pay(q):
        return pltpu.make_async_remote_copy(
            src_ref=send_v.at[q], dst_ref=recv_ref.at[me], send_sem=pay_send, recv_sem=pay_recv,
            device_id=(dom, q), device_id_type=MESH)

    def lab(q):
        return pltpu.make_async_remote_copy(
            src_ref=lab_v.at[q], dst_ref=lab_ref.at[me], send_sem=lab_send, recv_sem=lab_recv,
            device_id=(dom, q), device_id_type=MESH)

    lane = iota((1, L), 1)

    def fill(q):
        for s in range(CAP):
            send_v[q, s * R:(s + 1) * R, :] = term(tab_s[s, q]).astype(BF16)
        lab_v[q] = jnp.where(lane == 0, tab_s[2, q], tab_s[3, q])

    ring = (y + 3) & 7

    def send(n, c):
        half, i = n >> 3, n & 7
        away = jnp.where((i & 1) == 1, (i + 1) >> 1, 7 - (i >> 1))
        to_y = jnp.where(i == 7, 4, (5 + lax.rem(ring + away, 7)) & 7)
        peers = []
        for j in range(4):
            to_x, to_core = (x + half * 2 + j // 2) & 3, (core + j) & 1
            peers.append((to_x * 8 + to_y) * 2 + to_core)
        for q in peers:
            fill(q)

        @pl.when((n == 7) & (kind == 0))
        def _():
            pl.semaphore_wait(late.at[0], 8)

        for q in peers:
            @pl.when((q != me) & ((dom > 0) | (q > 0)))
            def _():
                pay(q).start()
                lab(q).start()
        return c

    lax.fori_loop(0, 16, send, 0)

    @pl.when((dom == 0) & (me > 0))
    def _():
        pl.semaphore_wait(late.at[1], 1)
        pay(0).start()
        lab(0).start()

    def at_home(i, acc):
        n = i * 8
        terms = []
        for j in range(8):
            pos = n + j
            terms.append(term(tab_s[4 + (pos >> 7), pos & 127]))
        for j in range(8):
            pos = n + j
            prev = jnp.maximum(pos - 1, 0)
            same = (tab_s[6 + (pos >> 7), pos & 127] == tab_s[6 + (prev >> 7), prev & 127]).astype(F32)
            acc = acc * same + terms[j]
            acc_v[pos] = acc
        return acc

    lax.fori_loop(0, UNITS // 8, at_home, jnp.zeros((R, L), F32))

    def fetch(t, c):
        home_v[t] = acc_v[jnp.clip(tab_s[8, t], 0, UNITS - 1)] * tab_s[9, t].astype(F32)
        return c

    lax.fori_loop(0, CB, fetch, 0, unroll=4)
    home_copy = pltpu.make_async_copy(home_v, home_ref, small_sem.at[3])
    home_copy.start()

    def all_pay():
        return pltpu.make_async_remote_copy(
            src_ref=send_v.at[pl.ds(0, NG - 1)], dst_ref=recv_ref.at[pl.ds(0, NG - 1)], send_sem=pay_send,
            recv_sem=pay_recv, device_id=(dom, me ^ 1), device_id_type=MESH)

    def all_lab():
        return pltpu.make_async_remote_copy(
            src_ref=lab_v.at[pl.ds(0, NG - 1)], dst_ref=lab_ref.at[pl.ds(0, NG - 1)], send_sem=lab_send,
            recv_sem=lab_recv, device_id=(dom, me ^ 1), device_id_type=MESH)

    @pl.when(has_high)
    def _():
        halo(True).wait_send()

    @pl.when(has_low)
    def _():
        halo(False).wait_send()

    home_copy.wait()
    all_lab().wait()
    all_pay().wait()


def collect(recv_ref, lab_ref, home_ref, out_ref, recv_v, lab_s, acc, acc_b, turned, rsem, lsem, hsem):
    me = lax.axis_index("grp")
    lab_copy = pltpu.make_async_copy(lab_ref, lab_s, lsem)
    lab_copy.start()
    home_copy = pltpu.make_async_copy(home_ref, acc.at[pl.ds(0, CB)], hsem)
    home_copy.start()
    copies = [pltpu.make_async_copy(recv_ref.at[pl.ds(i * 16, 16)], recv_v.at[pl.ds(i * 16, 16)], rsem.at[i]) for i in range(4)]
    for c in copies:
        c.start()
    acc_b[...] = jnp.zeros_like(acc_b)
    lab_copy.wait()
    home_copy.wait()

    def add(d, c):
        for s, total in ((0, acc), (1, acc_b)):
            t = jnp.where(d == me, CB, jnp.clip(lab_s[d, 0, s], 0, CB))
            total[t] = total[t] + recv_v[d, s * R:(s + 1) * R, :].astype(F32)
        return c

    for i in range(4):
        copies[i].wait()
        lax.fori_loop(i * 16, i * 16 + 16, add, 0, unroll=8)

    def turn(t, c):
        turned[pl.ds(t, R, stride=CB), :] = acc[t] + acc_b[t]
        return c

    lax.fori_loop(0, CB, turn, 0, unroll=8)
    for r in range(R):
        out_ref[:, r * L:(r + 1) * L] = turned[r * CB:(r + 1) * CB, :]


def on_device(a_blocks, p_blocks, columns, targets):
    hbm = pl.BlockSpec(memory_space=pl.ANY)
    dma = pltpu.SemaphoreType.DMA
    recv, labels, home = pl.pallas_call(
        exchange,
        out_shape=(
            jax.ShapeDtypeStruct((NG, CAP * R, L), BF16),
            jax.ShapeDtypeStruct((NG, 1, L), I32),
            jax.ShapeDtypeStruct((CB, R, L), F32),
        ),
        in_specs=[hbm] * 4,
        out_specs=(hbm, hbm, hbm),
        scratch_shapes=[
            pltpu.VMEM((K, E, 64 * 64), BF16),
            pltpu.VMEM((E, 64 * 64), BF16),
            pltpu.SMEM((K, E), I32),
            pltpu.VMEM((K, E), I32),
            pltpu.VMEM((16, L), I32),
            pltpu.SMEM((16, L), I32),
            pltpu.VMEM((R * E + E, L), F32),
            pltpu.VMEM((NP, R, L), BF16),
            pltpu.VMEM((NP, L, 2 * L), BF16),
            pltpu.VMEM((E, R, L), BF16),
            pltpu.VMEM((R * E + E, L), F32),
            pltpu.VMEM((UNITS, R, L), BF16),
            pltpu.VMEM((NG, CAP * R, L), BF16),
            pltpu.VMEM((NG, 1, L), I32),
            pltpu.VMEM((E * K, R, L), F32),
            pltpu.VMEM((CB, R, L), F32),
            dma((K,)), dma, dma((4,)), dma((2,)), dma((2,)), dma, dma, dma, dma,
            pltpu.SemaphoreType.REGULAR((2,)), pltpu.SemaphoreType.REGULAR,
        ],
        compiler_params=pltpu.CompilerParams(
            collective_id=0, has_side_effects=True, vmem_limit_bytes=62 * 1024 * 1024),
    )(a_blocks.transpose(1, 0, 2), p_blocks, columns.T, targets.T)
    return pl.pallas_call(
        collect,
        out_shape=jax.ShapeDtypeStruct((CB, 64 * 64), F32),
        in_specs=[hbm] * 3,
        out_specs=pl.BlockSpec(memory_space=pltpu.VMEM),
        scratch_shapes=[
            pltpu.VMEM((NG, CAP * R, L), BF16),
            pltpu.SMEM((NG, 1, L), I32),
            pltpu.VMEM((CB + 1, R, L), F32),
            pltpu.VMEM((CB + 1, R, L), F32),
            pltpu.VMEM((R * CB + CB, L), F32),
            dma((4,)), dma, dma,
        ],
        compiler_params=pltpu.CompilerParams(vmem_limit_bytes=62 * 1024 * 1024),
    )(recv, labels, home)


def solution(mesh):
    spec = P(("dom", "grp"), None)
    return jax.shard_map(
        on_device, mesh=mesh, in_specs=(P(("dom", "grp"), None, None), spec, spec, spec), out_specs=spec,
        check_vma=False)
```

```python
import functools

import jax
import jax.numpy as jnp
from jax import lax
from jax.experimental import pallas as pl
from jax.experimental.pallas import tpu as pltpu
from jax.sharding import PartitionSpec as P

MESH = pl.DeviceIdType.MESH
F32 = jnp.float32
BF16 = jnp.bfloat16
I32 = jnp.int32

E = 24
K = 7
HALO = 6
CB = 32
CAP = 2
NG = 64
R = 32
L = 128
UNITS = E * K
NP = E + 2 * HALO


def iota(shape, dim):
    return lax.broadcasted_iota(I32, shape, dim)


def split(u):
    k = (u * 2731) >> 16
    return k, u - k * E


def kind_of(dom, g):
    y = (g >> 1) & 7
    return jnp.where((dom == 0) & (g == 0), 7, jnp.where(y < 4, y, 10 - y))


def routing(tgt_v, device):
    t = tgt_v[...]
    owner = t >> 5
    col = t & (CB - 1)
    home = owner == device
    dest = jnp.where(home, NG, owner & (NG - 1)).astype(F32)
    key = jnp.where(home, col, CB).astype(F32)
    colf = col.astype(F32)
    unit_k, unit_e = split(iota((UNITS, K), 0)), split(iota((UNITS, E), 0))
    spread = jnp.where(unit_k[0] == iota((UNITS, K), 1), 1.0, 0.0).astype(F32)
    mine = unit_e[1] == iota((UNITS, E), 1)

    def column(x):
        wide = jnp.dot(spread, x, preferred_element_type=F32)
        return jnp.sum(jnp.where(mine, wide, 0.0), axis=1, keepdims=True)

    dest_c = column(dest)
    key_c = column(key)
    col_c = column(colf)
    pick = jnp.where(split(iota((E, UNITS), 1))[1] == iota((E, UNITS), 0), 1.0, 0.0).astype(F32)
    wide = jnp.dot(key, pick, preferred_element_type=F32)
    mine_r = split(iota((K, UNITS), 1))[0] == iota((K, UNITS), 0)
    key_r = jnp.sum(jnp.where(mine_r, wide, 0.0), axis=0, keepdims=True)
    unit_c = iota((UNITS, 1), 0).astype(F32)
    chosen = dest_c == iota((UNITS, L), 1).astype(F32)
    chosen = jnp.where(iota((UNITS, L), 1) < NG, jnp.where(chosen, 1.0, 0.0), 0.0)
    before = jnp.where(iota((UNITS, UNITS), 1) < iota((UNITS, UNITS), 0), 1.0, 0.0)
    rank = jnp.dot(before.astype(BF16), chosen.astype(BF16), preferred_element_type=F32)
    first = jnp.where(rank == 0.0, chosen, 0.0)
    second = jnp.where(rank == 1.0, chosen, 0.0)

    def row(x):
        return jnp.sum(x, axis=0, keepdims=True)

    rows = [
        row(first * unit_c),
        row(second * unit_c),
        row(first * (col_c - CB)) + CB,
        row(second * (col_c - CB)) + CB,
    ]
    full_c = key_c * 256.0 + unit_c
    full_r = key_r * 256.0 + iota((1, UNITS), 1).astype(F32)
    rank_c = jnp.sum(jnp.where(full_r < full_c, 1.0, 0.0), axis=1, keepdims=True)
    at = jnp.where(rank_c == iota((UNITS, 2 * L), 1).astype(F32), 1.0, 0.0)
    perm = row(at * unit_c)
    skey = row(at * key_c)
    slot = iota((UNITS, L), 1).astype(F32)
    upto = row(jnp.where(key_c <= slot, 1.0, 0.0))
    count = row(jnp.where(key_c == slot, 1.0, 0.0))
    rows += [perm[:, :L], perm[:, L:], skey[:, :L], skey[:, L:], jnp.maximum(upto - 1.0, 0.0), jnp.minimum(count, 1.0)]
    rows += [jnp.zeros((1, L), F32)] * (16 - len(rows))
    return jnp.concatenate(rows, axis=0).astype(I32)


def exchange(a_ref, p_ref, col_ref, tgt_ref, recv_ref, lab_ref, home_ref,
             a_v, p_v, col_s, tgt_v, tab_v, tab_s, pf, p2, w, ptx, af, a2,
             send_v, lab_v, acc_v, home_v,
             a_sem, p_sem, small_sem, halo_send, halo_recv, pay_send, pay_recv, lab_send, lab_recv, late, late_z):
    dom, me = lax.axis_index("dom"), lax.axis_index("grp")
    doms = lax.axis_size("dom")
    device = dom * NG + me
    x, y, core = me >> 4, (me >> 1) & 7, me & 1
    kind = kind_of(dom, me)
    has_low = dom > 0
    has_high = dom < doms - 1
    above_first = (dom == 1) & (me == 0)

    p_copy = pltpu.make_async_copy(p_ref, p_v, p_sem)
    p_copy.start()

    barrier = pltpu.get_barrier_semaphore()

    @pl.when(has_low)
    def _():
        pl.semaphore_signal(barrier, inc=1, device_id=(dom - 1, me), device_id_type=MESH)

    @pl.when(has_high & (kind < 7))
    def _():
        pl.semaphore_signal(barrier, inc=1, device_id=(dom + 1, me), device_id_type=MESH)

    def greet(d, c):
        q = (me + d) & (NG - 1)

        @pl.when(kind <= kind_of(dom, q))
        def _():
            pl.semaphore_signal(barrier, inc=1, device_id=(dom, q), device_id_type=MESH)

        return c

    lax.fori_loop(1, NG, greet, 0)

    tgt_copy = pltpu.make_async_copy(tgt_ref, tgt_v, small_sem.at[0])
    tgt_copy.start()
    col_copy = pltpu.make_async_copy(col_ref, col_s, small_sem.at[1])
    col_copy.start()
    a_copies = [pltpu.make_async_copy(a_ref.at[i], a_v.at[i], a_sem.at[i]) for i in range(K)]
    for c in a_copies:
        c.start()

    p_copy.wait()
    for r in range(R):
        pf[pl.ds(r * E, E), :] = p_v[:, r * L:(r + 1) * L].astype(F32)

    def own(e, c):
        p2[HALO + e] = pf[pl.ds(e, R, stride=E), :].astype(BF16)
        return c

    lax.fori_loop(0, E, own, 0, unroll=8)

    @pl.when(jnp.logical_not(has_low))
    def _():
        p2[pl.ds(0, HALO)] = jnp.zeros((HALO, R, L), BF16)

    @pl.when(jnp.logical_not(has_high))
    def _():
        p2[pl.ds(HALO + E, HALO)] = jnp.zeros((HALO, R, L), BF16)

    def halo(up):
        src = p2.at[pl.ds(E, HALO)] if up else p2.at[pl.ds(HALO, HALO)]
        dst = p2.at[pl.ds(0, HALO)] if up else p2.at[pl.ds(HALO + E, HALO)]
        i = 0 if up else 1
        return pltpu.make_async_remote_copy(
            src_ref=src, dst_ref=dst, send_sem=halo_send.at[i], recv_sem=halo_recv.at[i],
            device_id=(dom + 1 if up else dom - 1, me), device_id_type=MESH)

    rows = jnp.where(kind < 3, kind + 1, kind + 2)
    peers = jnp.where(kind == 7, NG - 1, rows * 8 - 1 - (dom == 0).astype(I32))
    low = (has_low & jnp.logical_not(above_first)).astype(I32)
    pl.semaphore_wait(barrier, peers + low + has_high.astype(I32))

    @pl.when(has_high)
    def _():
        halo(True).start()

    @pl.when(kind == 7)
    def _():
        pl.semaphore_signal(late_z, inc=1, device_id=(dom + 1, me), device_id_type=MESH)

    @pl.when(has_low & jnp.logical_not(above_first))
    def _():
        halo(False).start()

    here = jnp.where(kind == 7, 8, y)

    def answer(d, c):
        q = (me + d) & (NG - 1)

        @pl.when(kind_of(dom, q) < kind)
        def _():
            pl.semaphore_signal(late.at[here], inc=1, device_id=(dom, q), device_id_type=MESH)

        return c

    lax.fori_loop(1, NG, answer, 0)

    tgt_copy.wait()
    tab_v[...] = routing(tgt_v, device)
    tab_copy = pltpu.make_async_copy(tab_v, tab_s, small_sem.at[2])
    tab_copy.start()

    left = iota((R, L), 1) < 64
    row64, col64 = iota((64, 64), 0), iota((64, 64), 1)
    woven = jnp.where(row64 == ((col64 & 31) << 1) + (col64 >> 5), 1.0, 0.0).astype(BF16)
    even = jnp.where(iota((R, L), 1) == iota((R, L), 0) * 2, 1.0, 0.0).astype(BF16)

    def spread_block(c, b):
        br = pltpu.roll(b, 64, 1)
        parts = jnp.concatenate(
            [jnp.concatenate([jnp.where(left, b, 0.0), jnp.where(left, 0.0, br)], axis=1),
             jnp.concatenate([jnp.where(left, br, 0.0), jnp.where(left, 0.0, b)], axis=1)], axis=0).astype(BF16)
        z = jnp.dot(woven, parts, preferred_element_type=F32).astype(BF16)
        w[c, 0:64, :] = z
        w[c, 64:128, 0:L] = z[:, L:]
        w[c, 64:128, L:2 * L] = z[:, :L]

    def prepare(e, c):
        b = pf[pl.ds(e, R, stride=E), :]
        spread_block(HALO + e, b)
        stacked = jnp.concatenate(
            [b, pltpu.roll(b, 63, 1), pltpu.roll(b, 64, 1), pltpu.roll(b, 127, 1)], axis=0).astype(BF16)
        ptx[e] = lax.dot_general(
            even, stacked, (((1,), (1,)), ((), ())), preferred_element_type=F32).astype(BF16)
        return c

    lax.fori_loop(0, E, prepare, 0, unroll=4)

    def unpack(k, c):
        for r in range(R):
            af[pl.ds(r * E, E), :] = a_v[k, :, r * L:(r + 1) * L].astype(F32)
        for e in range(E):
            a2[k * E + e] = af[pl.ds(e, R, stride=E), :].astype(BF16)
        return c

    for i in range(K):
        a_copies[i].wait()
    lax.fori_loop(0, K, unpack, 0)
    col_copy.wait()
    tab_copy.wait()

    @pl.when(above_first)
    def _():
        pl.semaphore_wait(late_z, 1)
        halo(False).start()

    @pl.when(has_low)
    def _():
        halo(True).wait_recv()

    @pl.when(has_high)
    def _():
        halo(False).wait_recv()

    def prepare_halo(i, c):
        at = jnp.where(i < HALO, i, i + E)
        spread_block(at, p2[at].astype(F32))
        return c

    lax.fori_loop(0, 2 * HALO, prepare_halo, 0, unroll=4)

    first_own = device * E

    def term(u):
        u = jnp.clip(u, 0, UNITS - 1)
        k, e = split(u)
        rel = col_s[k, e] - first_own
        at = jnp.where(rel < 0, rel + NG * E - (E - HALO), jnp.where(rel < E, rel + HALO, rel - NG * E + HALO + E))
        at = jnp.clip(at, 0, NP - 1)
        out = jnp.dot(a2[u], w[at], preferred_element_type=F32)
        one, two = out[:, :L], out[:, L:]
        right = jnp.concatenate(
            [jnp.where(left, one, 0.0), jnp.where(left, 0.0, one),
             jnp.where(left, two, 0.0), jnp.where(left, 0.0, two)], axis=0).astype(BF16)
        return jnp.dot(ptx[e], right, preferred_element_type=F32)

    def pay(q):
        return pltpu.make_async_remote_copy(
            src_ref=send_v.at[q], dst_ref=recv_ref.at[me], send_sem=pay_send, recv_sem=pay_recv,
            device_id=(dom, q), device_id_type=MESH)

    def lab(q):
        return pltpu.make_async_remote_copy(
            src_ref=lab_v.at[q], dst_ref=lab_ref.at[me], send_sem=lab_send, recv_sem=lab_recv,
            device_id=(dom, q), device_id_type=MESH)

    lane = iota((1, L), 1)

    def fill(q):
        for s in range(CAP):
            send_v[q, s * R:(s + 1) * R, :] = term(tab_s[s, q]).astype(BF16)
        lab_v[q] = jnp.where(lane == 0, tab_s[2, q], tab_s[3, q])

    def send(n, c):
        turn, pair = n >> 2, n & 3
        dx = (2 - turn) & 3
        dx = jnp.where(turn == 2, 3, jnp.where(turn == 3, 0, dx))
        pair = jnp.where(turn == 0, (pair + 1) & 3, pair)
        to_ys = []
        for j, far in enumerate(((y + 4 + pair) & 7, (y + 3 - pair) & 7)):
            i = pair * 2 + j
            away = jnp.where(i == 0, 2, jnp.where(i == 1, 3, jnp.where(i == 2, 1, jnp.where(i == 3, 4, 0))))
            by_kind = jnp.where(i > 4, 11 - i, (7 + lax.rem(((y + 1) & 7) + away, 5)) & 7)
            to_ys.append(jnp.where(turn >= 2, by_kind, far))
        peers = [(((x + dx) & 3) * 8 + to_y) * 2 + ((core + j) & 1) for to_y in to_ys for j in range(2)]
        for q in peers:
            fill(q)

        for to_y in to_ys:
            @pl.when((n < 4) & (jnp.where(to_y < 4, to_y, 10 - to_y) > kind))
            def _():
                pl.semaphore_wait(late.at[to_y], 8)

        for q in peers:
            @pl.when((q != me) & ((dom > 0) | (q > 0)))
            def _():
                pay(q).start()
                lab(q).start()
        return c

    lax.fori_loop(0, 16, send, 0)

    @pl.when((dom == 0) & (me > 0))
    def _():
        pl.semaphore_wait(late.at[8], 1)
        pay(0).start()
        lab(0).start()

    def at_home(i, acc):
        n = i * 8
        terms = []
        for j in range(8):
            pos = n + j
            terms.append(term(tab_s[4 + (pos >> 7), pos & 127]))
        for j in range(8):
            pos = n + j
            prev = jnp.maximum(pos - 1, 0)
            same = (tab_s[6 + (pos >> 7), pos & 127] == tab_s[6 + (prev >> 7), prev & 127]).astype(F32)
            acc = acc * same + terms[j]
            acc_v[pos] = acc
        return acc

    lax.fori_loop(0, UNITS // 8, at_home, jnp.zeros((R, L), F32))

    def fetch(t, c):
        home_v[t] = acc_v[jnp.clip(tab_s[8, t], 0, UNITS - 1)] * tab_s[9, t].astype(F32)
        return c

    lax.fori_loop(0, CB, fetch, 0, unroll=4)
    home_copy = pltpu.make_async_copy(home_v, home_ref, small_sem.at[3])
    home_copy.start()

    def all_pay():
        return pltpu.make_async_remote_copy(
            src_ref=send_v.at[pl.ds(0, NG - 1)], dst_ref=recv_ref.at[pl.ds(0, NG - 1)], send_sem=pay_send,
            recv_sem=pay_recv, device_id=(dom, me ^ 1), device_id_type=MESH)

    def all_lab():
        return pltpu.make_async_remote_copy(
            src_ref=lab_v.at[pl.ds(0, NG - 1)], dst_ref=lab_ref.at[pl.ds(0, NG - 1)], send_sem=lab_send,
            recv_sem=lab_recv, device_id=(dom, me ^ 1), device_id_type=MESH)

    @pl.when(has_high)
    def _():
        halo(True).wait_send()

    @pl.when(has_low)
    def _():
        halo(False).wait_send()

    home_copy.wait()
    all_lab().wait()
    all_pay().wait()


def collect(recv_ref, lab_ref, home_ref, out_ref, recv_v, lab_s, acc, acc_b, turned, rsem, lsem, hsem):
    me = lax.axis_index("grp")
    lab_copy = pltpu.make_async_copy(lab_ref, lab_s, lsem)
    lab_copy.start()
    home_copy = pltpu.make_async_copy(home_ref, acc.at[pl.ds(0, CB)], hsem)
    home_copy.start()
    copies = [pltpu.make_async_copy(recv_ref.at[pl.ds(i * 16, 16)], recv_v.at[pl.ds(i * 16, 16)], rsem.at[i]) for i in range(4)]
    for c in copies:
        c.start()
    acc_b[...] = jnp.zeros_like(acc_b)
    lab_copy.wait()
    home_copy.wait()

    def add(d, c):
        for s, total in ((0, acc), (1, acc_b)):
            t = jnp.where(d == me, CB, jnp.clip(lab_s[d, 0, s], 0, CB))
            total[t] = total[t] + recv_v[d, s * R:(s + 1) * R, :].astype(F32)
        return c

    for i in range(4):
        copies[i].wait()
        lax.fori_loop(i * 16, i * 16 + 16, add, 0, unroll=8)

    def turn(t, c):
        turned[pl.ds(t, R, stride=CB), :] = acc[t] + acc_b[t]
        return c

    lax.fori_loop(0, CB, turn, 0, unroll=8)
    for r in range(R):
        out_ref[:, r * L:(r + 1) * L] = turned[r * CB:(r + 1) * CB, :]


def on_device(a_blocks, p_blocks, columns, targets):
    hbm = pl.BlockSpec(memory_space=pl.ANY)
    dma = pltpu.SemaphoreType.DMA
    recv, labels, home = pl.pallas_call(
        exchange,
        out_shape=(
            jax.ShapeDtypeStruct((NG, CAP * R, L), BF16),
            jax.ShapeDtypeStruct((NG, 1, L), I32),
            jax.ShapeDtypeStruct((CB, R, L), F32),
        ),
        in_specs=[hbm] * 4,
        out_specs=(hbm, hbm, hbm),
        scratch_shapes=[
            pltpu.VMEM((K, E, 64 * 64), BF16),
            pltpu.VMEM((E, 64 * 64), BF16),
            pltpu.SMEM((K, E), I32),
            pltpu.VMEM((K, E), I32),
            pltpu.VMEM((16, L), I32),
            pltpu.SMEM((16, L), I32),
            pltpu.VMEM((R * E + E, L), F32),
            pltpu.VMEM((NP, R, L), BF16),
            pltpu.VMEM((NP, L, 2 * L), BF16),
            pltpu.VMEM((E, R, L), BF16),
            pltpu.VMEM((R * E + E, L), F32),
            pltpu.VMEM((UNITS, R, L), BF16),
            pltpu.VMEM((NG, CAP * R, L), BF16),
            pltpu.VMEM((NG, 1, L), I32),
            pltpu.VMEM((E * K, R, L), F32),
            pltpu.VMEM((CB, R, L), F32),
            dma((K,)), dma, dma((4,)), dma((2,)), dma((2,)), dma, dma, dma, dma,
            pltpu.SemaphoreType.REGULAR((9,)), pltpu.SemaphoreType.REGULAR,
        ],
        compiler_params=pltpu.CompilerParams(
            collective_id=0, has_side_effects=True, vmem_limit_bytes=62 * 1024 * 1024),
    )(a_blocks.transpose(1, 0, 2), p_blocks, columns.T, targets.T)
    return pl.pallas_call(
        collect,
        out_shape=jax.ShapeDtypeStruct((CB, 64 * 64), F32),
        in_specs=[hbm] * 3,
        out_specs=pl.BlockSpec(memory_space=pltpu.VMEM),
        scratch_shapes=[
            pltpu.VMEM((NG, CAP * R, L), BF16),
            pltpu.SMEM((NG, 1, L), I32),
            pltpu.VMEM((CB + 1, R, L), F32),
            pltpu.VMEM((CB + 1, R, L), F32),
            pltpu.VMEM((R * CB + CB, L), F32),
            dma((4,)), dma, dma,
        ],
        compiler_params=pltpu.CompilerParams(vmem_limit_bytes=62 * 1024 * 1024),
    )(recv, labels, home)


def solution(mesh):
    spec = P(("dom", "grp"), None)
    return jax.shard_map(
        on_device, mesh=mesh, in_specs=(P(("dom", "grp"), None, None), spec, spec, spec), out_specs=spec,
        check_vma=False)
```

```python
import functools

import jax
import jax.numpy as jnp
from jax import lax
from jax.experimental import pallas as pl
from jax.experimental.pallas import tpu as pltpu
from jax.sharding import PartitionSpec as P

MESH = pl.DeviceIdType.MESH
F32 = jnp.float32
BF16 = jnp.bfloat16
I32 = jnp.int32

E = 24
K = 7
HALO = 6
CB = 32
CAP = 2
NG = 64
R = 32
L = 128
UNITS = E * K
NP = E + 2 * HALO


def iota(shape, dim):
    return lax.broadcasted_iota(I32, shape, dim)


def split(u):
    k = (u * 2731) >> 16
    return k, u - k * E


def kind_of(dom, g):
    y = (g >> 1) & 7
    return jnp.where((dom == 0) & (g == 0), 7, jnp.where(y < 4, y, 10 - y))


def routing(tgt_v, device):
    t = tgt_v[...]
    owner = t >> 5
    col = t & (CB - 1)
    home = owner == device
    dest = jnp.where(home, NG, owner & (NG - 1)).astype(F32)
    key = jnp.where(home, col, CB).astype(F32)
    colf = col.astype(F32)
    unit_k, unit_e = split(iota((UNITS, K), 0)), split(iota((UNITS, E), 0))
    spread = jnp.where(unit_k[0] == iota((UNITS, K), 1), 1.0, 0.0).astype(F32)
    mine = unit_e[1] == iota((UNITS, E), 1)

    def column(x):
        wide = jnp.dot(spread, x, preferred_element_type=F32)
        return jnp.sum(jnp.where(mine, wide, 0.0), axis=1, keepdims=True)

    dest_c = column(dest)
    key_c = column(key)
    col_c = column(colf)
    pick = jnp.where(split(iota((E, UNITS), 1))[1] == iota((E, UNITS), 0), 1.0, 0.0).astype(F32)
    wide = jnp.dot(key, pick, preferred_element_type=F32)
    mine_r = split(iota((K, UNITS), 1))[0] == iota((K, UNITS), 0)
    key_r = jnp.sum(jnp.where(mine_r, wide, 0.0), axis=0, keepdims=True)
    unit_c = iota((UNITS, 1), 0).astype(F32)
    chosen = dest_c == iota((UNITS, L), 1).astype(F32)
    chosen = jnp.where(iota((UNITS, L), 1) < NG, jnp.where(chosen, 1.0, 0.0), 0.0)
    before = jnp.where(iota((UNITS, UNITS), 1) < iota((UNITS, UNITS), 0), 1.0, 0.0)
    rank = jnp.dot(before.astype(BF16), chosen.astype(BF16), preferred_element_type=F32)
    first = jnp.where(rank == 0.0, chosen, 0.0)
    second = jnp.where(rank == 1.0, chosen, 0.0)

    def row(x):
        return jnp.sum(x, axis=0, keepdims=True)

    rows = [
        row(first * unit_c),
        row(second * unit_c),
        row(first * (col_c - CB)) + CB,
        row(second * (col_c - CB)) + CB,
    ]
    full_c = key_c * 256.0 + unit_c
    full_r = key_r * 256.0 + iota((1, UNITS), 1).astype(F32)
    rank_c = jnp.sum(jnp.where(full_r < full_c, 1.0, 0.0), axis=1, keepdims=True)
    at = jnp.where(rank_c == iota((UNITS, 2 * L), 1).astype(F32), 1.0, 0.0)
    perm = row(at * unit_c)
    skey = row(at * key_c)
    slot = iota((UNITS, L), 1).astype(F32)
    upto = row(jnp.where(key_c <= slot, 1.0, 0.0))
    count = row(jnp.where(key_c == slot, 1.0, 0.0))
    rows += [perm[:, :L], perm[:, L:], skey[:, :L], skey[:, L:], jnp.maximum(upto - 1.0, 0.0), jnp.minimum(count, 1.0)]
    rows += [jnp.zeros((1, L), F32)] * (16 - len(rows))
    return jnp.concatenate(rows, axis=0).astype(I32)


def exchange(a_ref, p_ref, col_ref, tgt_ref, recv_ref, lab_ref, home_ref,
             a_v, p_v, col_s, tgt_v, tab_v, tab_s, pf, p2, w, ptx, af, a2,
             send_v, lab_v, acc_v, home_v,
             a_sem, p_sem, small_sem, halo_send, halo_recv, pay_send, pay_recv, lab_send, lab_recv, late, late_z):
    dom, me = lax.axis_index("dom"), lax.axis_index("grp")
    doms = lax.axis_size("dom")
    device = dom * NG + me
    x, y, core = me >> 4, (me >> 1) & 7, me & 1
    kind = kind_of(dom, me)
    has_low = dom > 0
    has_high = dom < doms - 1
    above_first = (dom == 1) & (me == 0)

    half = 64 * 64 // 2
    p_copies = [
        pltpu.make_async_copy(p_ref.at[:, pl.ds(i * half, half)], p_v.at[:, pl.ds(i * half, half)], p_sem.at[i])
        for i in range(2)
    ]
    for c in p_copies:
        c.start()

    barrier = pltpu.get_barrier_semaphore()

    @pl.when(has_low)
    def _():
        pl.semaphore_signal(barrier, inc=1, device_id=(dom - 1, me), device_id_type=MESH)

    @pl.when(has_high & (kind < 7))
    def _():
        pl.semaphore_signal(barrier, inc=1, device_id=(dom + 1, me), device_id_type=MESH)

    def greet(d, c):
        q = (me + d) & (NG - 1)

        @pl.when(kind <= kind_of(dom, q))
        def _():
            pl.semaphore_signal(barrier, inc=1, device_id=(dom, q), device_id_type=MESH)

        return c

    lax.fori_loop(1, NG, greet, 0)

    tgt_copy = pltpu.make_async_copy(tgt_ref, tgt_v, small_sem.at[0])
    tgt_copy.start()
    col_copy = pltpu.make_async_copy(col_ref, col_s, small_sem.at[1])
    col_copy.start()
    a_copies = [pltpu.make_async_copy(a_ref.at[i], a_v.at[i], a_sem.at[i]) for i in range(K)]
    for c in a_copies:
        c.start()

    for r in range(R):
        if r % (R // 2) == 0:
            p_copies[r // (R // 2)].wait()
        pf[pl.ds(r * E, E), :] = p_v[:, r * L:(r + 1) * L].astype(F32)
    for e in [*range(HALO), *range(E - HALO, E)]:
        p2[HALO + e] = pf[pl.ds(e, R, stride=E), :].astype(BF16)

    @pl.when(jnp.logical_not(has_low))
    def _():
        p2[pl.ds(0, HALO)] = jnp.zeros((HALO, R, L), BF16)

    @pl.when(jnp.logical_not(has_high))
    def _():
        p2[pl.ds(HALO + E, HALO)] = jnp.zeros((HALO, R, L), BF16)

    def halo(up):
        src = p2.at[pl.ds(E, HALO)] if up else p2.at[pl.ds(HALO, HALO)]
        dst = p2.at[pl.ds(0, HALO)] if up else p2.at[pl.ds(HALO + E, HALO)]
        i = 0 if up else 1
        return pltpu.make_async_remote_copy(
            src_ref=src, dst_ref=dst, send_sem=halo_send.at[i], recv_sem=halo_recv.at[i],
            device_id=(dom + 1 if up else dom - 1, me), device_id_type=MESH)

    rows = jnp.where(kind < 3, kind + 1, kind + 2)
    peers = jnp.where(kind == 7, NG - 1, rows * 8 - 1 - (dom == 0).astype(I32))
    low = (has_low & jnp.logical_not(above_first)).astype(I32)
    pl.semaphore_wait(barrier, peers + low + has_high.astype(I32))

    @pl.when(has_high)
    def _():
        halo(True).start()

    @pl.when(kind == 7)
    def _():
        pl.semaphore_signal(late_z, inc=1, device_id=(dom + 1, me), device_id_type=MESH)

    @pl.when(has_low & jnp.logical_not(above_first))
    def _():
        halo(False).start()

    here = jnp.where(kind == 7, 8, y)

    def answer(d, c):
        q = (me + d) & (NG - 1)

        @pl.when(kind_of(dom, q) < kind)
        def _():
            pl.semaphore_signal(late.at[here], inc=1, device_id=(dom, q), device_id_type=MESH)

        return c

    lax.fori_loop(1, NG, answer, 0)

    tgt_copy.wait()
    tab_v[...] = routing(tgt_v, device)
    tab_copy = pltpu.make_async_copy(tab_v, tab_s, small_sem.at[2])
    tab_copy.start()

    left = iota((R, L), 1) < 64
    row64, col64 = iota((64, 64), 0), iota((64, 64), 1)
    woven = jnp.where(row64 == ((col64 & 31) << 1) + (col64 >> 5), 1.0, 0.0).astype(BF16)
    even = jnp.where(iota((R, L), 1) == iota((R, L), 0) * 2, 1.0, 0.0).astype(BF16)

    def spread_block(c, b):
        br = pltpu.roll(b, 64, 1)
        parts = jnp.concatenate(
            [jnp.concatenate([jnp.where(left, b, 0.0), jnp.where(left, 0.0, br)], axis=1),
             jnp.concatenate([jnp.where(left, br, 0.0), jnp.where(left, 0.0, b)], axis=1)], axis=0).astype(BF16)
        z = jnp.dot(woven, parts, preferred_element_type=F32).astype(BF16)
        w[c, 0:64, :] = z
        w[c, 64:128, 0:L] = z[:, L:]
        w[c, 64:128, L:2 * L] = z[:, :L]

    def prepare(e, c):
        b = pf[pl.ds(e, R, stride=E), :]
        spread_block(HALO + e, b)
        stacked = jnp.concatenate(
            [b, pltpu.roll(b, 63, 1), pltpu.roll(b, 64, 1), pltpu.roll(b, 127, 1)], axis=0).astype(BF16)
        ptx[e] = lax.dot_general(
            even, stacked, (((1,), (1,)), ((), ())), preferred_element_type=F32).astype(BF16)
        return c

    lax.fori_loop(0, E, prepare, 0, unroll=4)

    def unpack(k, c):
        for r in range(R):
            af[pl.ds(r * E, E), :] = a_v[k, :, r * L:(r + 1) * L].astype(F32)
        for e in range(E):
            a2[k * E + e] = af[pl.ds(e, R, stride=E), :].astype(BF16)
        return c

    for i in range(K):
        a_copies[i].wait()
    lax.fori_loop(0, K, unpack, 0)
    col_copy.wait()
    tab_copy.wait()

    @pl.when(above_first)
    def _():
        pl.semaphore_wait(late_z, 1)
        halo(False).start()

    @pl.when(has_low)
    def _():
        halo(True).wait_recv()

    @pl.when(has_high)
    def _():
        halo(False).wait_recv()

    def prepare_halo(i, c):
        at = jnp.where(i < HALO, i, i + E)
        spread_block(at, p2[at].astype(F32))
        return c

    lax.fori_loop(0, 2 * HALO, prepare_halo, 0, unroll=12)

    first_own = device * E

    def term(u):
        u = jnp.clip(u, 0, UNITS - 1)
        k, e = split(u)
        rel = col_s[k, e] - first_own
        at = jnp.where(rel < 0, rel + NG * E - (E - HALO), jnp.where(rel < E, rel + HALO, rel - NG * E + HALO + E))
        at = jnp.clip(at, 0, NP - 1)
        out = jnp.dot(a2[u], w[at], preferred_element_type=F32)
        one, two = out[:, :L], out[:, L:]
        right = jnp.concatenate(
            [jnp.where(left, one, 0.0), jnp.where(left, 0.0, one),
             jnp.where(left, two, 0.0), jnp.where(left, 0.0, two)], axis=0).astype(BF16)
        return jnp.dot(ptx[e], right, preferred_element_type=F32)

    def pay(q):
        return pltpu.make_async_remote_copy(
            src_ref=send_v.at[q], dst_ref=recv_ref.at[me], send_sem=pay_send, recv_sem=pay_recv,
            device_id=(dom, q), device_id_type=MESH)

    def lab(q):
        return pltpu.make_async_remote_copy(
            src_ref=lab_v.at[q], dst_ref=lab_ref.at[me], send_sem=lab_send, recv_sem=lab_recv,
            device_id=(dom, q), device_id_type=MESH)

    lane = iota((1, L), 1)

    def fill(q):
        for s in range(CAP):
            send_v[q, s * R:(s + 1) * R, :] = term(tab_s[s, q]).astype(BF16)
        lab_v[q] = jnp.where(lane == 0, tab_s[2, q], tab_s[3, q])

    def send(n, c):
        turn, pair = n >> 2, n & 3
        dx = (2 - turn) & 3
        dx = jnp.where(turn == 2, 3, jnp.where(turn == 3, 0, dx))
        pair = jnp.where(turn == 0, (pair + 1) & 3, pair)
        to_ys = []
        for j, far in enumerate(((y + 4 + pair) & 7, (y + 3 - pair) & 7)):
            i = pair * 2 + j
            away = jnp.where(i == 0, 2, jnp.where(i == 1, 3, jnp.where(i == 2, 1, jnp.where(i == 3, 4, 0))))
            by_kind = jnp.where(i > 4, 11 - i, (7 + lax.rem(((y + 1) & 7) + away, 5)) & 7)
            to_ys.append(jnp.where(turn >= 2, by_kind, far))
        peers = [(((x + dx) & 3) * 8 + to_y) * 2 + ((core + j) & 1) for to_y in to_ys for j in range(2)]
        for q in peers:
            fill(q)

        for to_y in to_ys:
            @pl.when((n < 4) & (jnp.where(to_y < 4, to_y, 10 - to_y) > kind))
            def _():
                pl.semaphore_wait(late.at[to_y], 8)

        for q in peers:
            @pl.when((q != me) & ((dom > 0) | (q > 0)))
            def _():
                pay(q).start()
                lab(q).start()
        return c

    lax.fori_loop(0, 16, send, 0)

    @pl.when((dom == 0) & (me > 0))
    def _():
        pl.semaphore_wait(late.at[8], 1)
        pay(0).start()
        lab(0).start()

    def at_home(i, acc):
        n = i * 8
        terms = []
        for j in range(8):
            pos = n + j
            terms.append(term(tab_s[4 + (pos >> 7), pos & 127]))
        for j in range(8):
            pos = n + j
            prev = jnp.maximum(pos - 1, 0)
            same = (tab_s[6 + (pos >> 7), pos & 127] == tab_s[6 + (prev >> 7), prev & 127]).astype(F32)
            acc = acc * same + terms[j]
            acc_v[pos] = acc
        return acc

    lax.fori_loop(0, UNITS // 8, at_home, jnp.zeros((R, L), F32))

    def fetch(t, c):
        home_v[t] = acc_v[jnp.clip(tab_s[8, t], 0, UNITS - 1)] * tab_s[9, t].astype(F32)
        return c

    lax.fori_loop(0, CB, fetch, 0, unroll=4)
    home_copy = pltpu.make_async_copy(home_v, home_ref, small_sem.at[3])
    home_copy.start()

    def all_pay():
        return pltpu.make_async_remote_copy(
            src_ref=send_v.at[pl.ds(0, NG - 1)], dst_ref=recv_ref.at[pl.ds(0, NG - 1)], send_sem=pay_send,
            recv_sem=pay_recv, device_id=(dom, me ^ 1), device_id_type=MESH)

    def all_lab():
        return pltpu.make_async_remote_copy(
            src_ref=lab_v.at[pl.ds(0, NG - 1)], dst_ref=lab_ref.at[pl.ds(0, NG - 1)], send_sem=lab_send,
            recv_sem=lab_recv, device_id=(dom, me ^ 1), device_id_type=MESH)

    @pl.when(has_high)
    def _():
        halo(True).wait_send()

    @pl.when(has_low)
    def _():
        halo(False).wait_send()

    home_copy.wait()
    all_lab().wait()
    all_pay().wait()


def collect(recv_ref, lab_ref, home_ref, out_ref, recv_v, lab_s, acc, acc_b, turned, out_v, rsem, lsem, hsem, osem):
    me = lax.axis_index("grp")
    lab_copy = pltpu.make_async_copy(lab_ref, lab_s, lsem)
    lab_copy.start()
    home_copy = pltpu.make_async_copy(home_ref, acc.at[pl.ds(0, CB)], hsem)
    home_copy.start()
    copies = [pltpu.make_async_copy(recv_ref.at[pl.ds(i * 16, 16)], recv_v.at[pl.ds(i * 16, 16)], rsem.at[i]) for i in range(4)]
    for c in copies:
        c.start()
    acc_b[...] = jnp.zeros_like(acc_b)
    lab_copy.wait()
    home_copy.wait()

    def add(d, c):
        for s, total in ((0, acc), (1, acc_b)):
            t = jnp.where(d == me, CB, jnp.clip(lab_s[d, 0, s], 0, CB))
            total[t] = total[t] + recv_v[d, s * R:(s + 1) * R, :].astype(F32)
        return c

    for i in range(4):
        copies[i].wait()
        lax.fori_loop(i * 16, i * 16 + 16, add, 0, unroll=16)

    outs = []
    for g in range(0, CB, 8):
        for t in range(g, g + 8):
            turned[pl.ds(t, R, stride=CB), :] = acc[t] + acc_b[t]
        for r in range(R):
            out_v[g:g + 8, r * L:(r + 1) * L] = turned[r * CB + g:r * CB + g + 8, :]
        outs.append(pltpu.make_async_copy(out_v.at[pl.ds(g, 8)], out_ref.at[pl.ds(g, 8)], osem.at[g // 8]))
        outs[-1].start()
    for c in outs:
        c.wait()


def on_device(a_blocks, p_blocks, columns, targets):
    hbm = pl.BlockSpec(memory_space=pl.ANY)
    dma = pltpu.SemaphoreType.DMA
    recv, labels, home = pl.pallas_call(
        exchange,
        out_shape=(
            jax.ShapeDtypeStruct((NG, CAP * R, L), BF16),
            jax.ShapeDtypeStruct((NG, 1, L), I32),
            jax.ShapeDtypeStruct((CB, R, L), F32),
        ),
        in_specs=[hbm] * 4,
        out_specs=(hbm, hbm, hbm),
        scratch_shapes=[
            pltpu.VMEM((K, E, 64 * 64), BF16),
            pltpu.VMEM((E, 64 * 64), BF16),
            pltpu.SMEM((K, E), I32),
            pltpu.VMEM((K, E), I32),
            pltpu.VMEM((16, L), I32),
            pltpu.SMEM((16, L), I32),
            pltpu.VMEM((R * E + E, L), F32),
            pltpu.VMEM((NP, R, L), BF16),
            pltpu.VMEM((NP, L, 2 * L), BF16),
            pltpu.VMEM((E, R, L), BF16),
            pltpu.VMEM((R * E + E, L), F32),
            pltpu.VMEM((UNITS, R, L), BF16),
            pltpu.VMEM((NG, CAP * R, L), BF16),
            pltpu.VMEM((NG, 1, L), I32),
            pltpu.VMEM((E * K, R, L), F32),
            pltpu.VMEM((CB, R, L), F32),
            dma((K,)), dma((2,)), dma((4,)), dma((2,)), dma((2,)), dma, dma, dma, dma,
            pltpu.SemaphoreType.REGULAR((9,)), pltpu.SemaphoreType.REGULAR,
        ],
        compiler_params=pltpu.CompilerParams(
            collective_id=0, has_side_effects=True, vmem_limit_bytes=62 * 1024 * 1024),
    )(a_blocks.transpose(1, 0, 2), p_blocks, columns.T, targets.T)
    return pl.pallas_call(
        collect,
        out_shape=jax.ShapeDtypeStruct((CB, 64 * 64), F32),
        in_specs=[hbm] * 3,
        out_specs=hbm,
        scratch_shapes=[
            pltpu.VMEM((NG, CAP * R, L), BF16),
            pltpu.SMEM((NG, 1, L), I32),
            pltpu.VMEM((CB + 1, R, L), F32),
            pltpu.VMEM((CB + 1, R, L), F32),
            pltpu.VMEM((R * CB + CB, L), F32),
            pltpu.VMEM((CB, 64 * 64), F32),
            dma((4,)), dma, dma, dma((4,)),
        ],
        compiler_params=pltpu.CompilerParams(vmem_limit_bytes=62 * 1024 * 1024),
    )(recv, labels, home)


def solution(mesh):
    spec = P(("dom", "grp"), None)
    return jax.shard_map(
        on_device, mesh=mesh, in_specs=(P(("dom", "grp"), None, None), spec, spec, spec), out_specs=spec,
        check_vma=False)
```

```python
import functools

import jax
import jax.numpy as jnp
from jax import lax
from jax.experimental import pallas as pl
from jax.experimental.pallas import tpu as pltpu
from jax.sharding import PartitionSpec as P

MESH = pl.DeviceIdType.MESH
F32 = jnp.float32
BF16 = jnp.bfloat16
I32 = jnp.int32

E = 24
K = 7
HALO = 6
CB = 32
CAP = 2
NG = 64
R = 32
L = 128
UNITS = E * K
NP = E + 2 * HALO


def iota(shape, dim):
    return lax.broadcasted_iota(I32, shape, dim)


def split(u):
    k = (u * 2731) >> 16
    return k, u - k * E


def kind_of(dom, g):
    y = (g >> 1) & 7
    return jnp.where((dom == 0) & (g == 0), 7, jnp.where(y < 4, y, 10 - y))


def routing(tgt_v, device):
    t = tgt_v[...]
    owner = t >> 5
    col = t & (CB - 1)
    home = owner == device
    dest = jnp.where(home, NG, owner & (NG - 1)).astype(F32)
    key = jnp.where(home, col, CB).astype(F32)
    colf = col.astype(F32)
    unit_k, unit_e = split(iota((UNITS, K), 0)), split(iota((UNITS, E), 0))
    spread = jnp.where(unit_k[0] == iota((UNITS, K), 1), 1.0, 0.0).astype(F32)
    mine = unit_e[1] == iota((UNITS, E), 1)

    def column(x):
        wide = jnp.dot(spread, x, preferred_element_type=F32)
        return jnp.sum(jnp.where(mine, wide, 0.0), axis=1, keepdims=True)

    dest_c = column(dest)
    key_c = column(key)
    col_c = column(colf)
    pick = jnp.where(split(iota((E, UNITS), 1))[1] == iota((E, UNITS), 0), 1.0, 0.0).astype(F32)
    wide = jnp.dot(key, pick, preferred_element_type=F32)
    mine_r = split(iota((K, UNITS), 1))[0] == iota((K, UNITS), 0)
    key_r = jnp.sum(jnp.where(mine_r, wide, 0.0), axis=0, keepdims=True)
    unit_c = iota((UNITS, 1), 0).astype(F32)
    chosen = dest_c == iota((UNITS, L), 1).astype(F32)
    chosen = jnp.where(iota((UNITS, L), 1) < NG, jnp.where(chosen, 1.0, 0.0), 0.0)
    before = jnp.where(iota((UNITS, UNITS), 1) < iota((UNITS, UNITS), 0), 1.0, 0.0)
    rank = jnp.dot(before.astype(BF16), chosen.astype(BF16), preferred_element_type=F32)
    first = jnp.where(rank == 0.0, chosen, 0.0)
    second = jnp.where(rank == 1.0, chosen, 0.0)

    def row(x):
        return jnp.sum(x, axis=0, keepdims=True)

    rows = [
        row(first * unit_c),
        row(second * unit_c),
        row(first * (col_c - CB)) + CB,
        row(second * (col_c - CB)) + CB,
    ]
    full_c = key_c * 256.0 + unit_c
    full_r = key_r * 256.0 + iota((1, UNITS), 1).astype(F32)
    rank_c = jnp.sum(jnp.where(full_r < full_c, 1.0, 0.0), axis=1, keepdims=True)
    at = jnp.where(rank_c == iota((UNITS, 2 * L), 1).astype(F32), 1.0, 0.0)
    perm = row(at * unit_c)
    skey = row(at * key_c)
    slot = iota((UNITS, L), 1).astype(F32)
    upto = row(jnp.where(key_c <= slot, 1.0, 0.0))
    count = row(jnp.where(key_c == slot, 1.0, 0.0))
    rows += [perm[:, :L], perm[:, L:], skey[:, :L], skey[:, L:], jnp.maximum(upto - 1.0, 0.0), jnp.minimum(count, 1.0)]
    rows += [jnp.zeros((1, L), F32)] * (16 - len(rows))
    return jnp.concatenate(rows, axis=0).astype(I32)


def exchange(a_ref, p_ref, col_ref, tgt_ref, recv_ref, lab_ref, home_ref,
             a_v, p_v, col_s, tgt_v, tab_v, tab_s, pf, p2, w, ptx, af, a2,
             send_v, lab_v, acc_v, home_v,
             a_sem, p_sem, small_sem, halo_send, halo_recv, pay_send, pay_recv, lab_send, lab_recv, late, late_z):
    dom, me = lax.axis_index("dom"), lax.axis_index("grp")
    doms = lax.axis_size("dom")
    device = dom * NG + me
    x, y, core = me >> 4, (me >> 1) & 7, me & 1
    kind = kind_of(dom, me)
    has_low = dom > 0
    has_high = dom < doms - 1
    above_first = (dom == 1) & (me == 0)

    half = 64 * 64 // 2
    p_copies = [
        pltpu.make_async_copy(p_ref.at[:, pl.ds(i * half, half)], p_v.at[:, pl.ds(i * half, half)], p_sem.at[i])
        for i in range(2)
    ]
    for c in p_copies:
        c.start()

    barrier = pltpu.get_barrier_semaphore()

    @pl.when(has_low)
    def _():
        pl.semaphore_signal(barrier, inc=1, device_id=(dom - 1, me), device_id_type=MESH)

    @pl.when(has_high & (kind < 7))
    def _():
        pl.semaphore_signal(barrier, inc=1, device_id=(dom + 1, me), device_id_type=MESH)

    def greet(d, c):
        q = (me + d) & (NG - 1)

        @pl.when(kind <= kind_of(dom, q))
        def _():
            pl.semaphore_signal(barrier, inc=1, device_id=(dom, q), device_id_type=MESH)

        return c

    lax.fori_loop(1, NG, greet, 0)

    tgt_copy = pltpu.make_async_copy(tgt_ref, tgt_v, small_sem.at[0])
    tgt_copy.start()
    col_copy = pltpu.make_async_copy(col_ref, col_s, small_sem.at[1])
    col_copy.start()
    a_copies = [pltpu.make_async_copy(a_ref.at[i], a_v.at[i], a_sem.at[i]) for i in range(K)]
    for c in a_copies:
        c.start()

    for r in range(R):
        if r % (R // 2) == 0:
            p_copies[r // (R // 2)].wait()
        pf[pl.ds(r * E, E), :] = p_v[:, r * L:(r + 1) * L].astype(F32)
    for e in [*range(HALO), *range(E - HALO, E)]:
        p2[HALO + e] = pf[pl.ds(e, R, stride=E), :].astype(BF16)

    @pl.when(jnp.logical_not(has_low))
    def _():
        p2[pl.ds(0, HALO)] = jnp.zeros((HALO, R, L), BF16)

    @pl.when(jnp.logical_not(has_high))
    def _():
        p2[pl.ds(HALO + E, HALO)] = jnp.zeros((HALO, R, L), BF16)

    def halo(up):
        src = p2.at[pl.ds(E, HALO)] if up else p2.at[pl.ds(HALO, HALO)]
        dst = p2.at[pl.ds(0, HALO)] if up else p2.at[pl.ds(HALO + E, HALO)]
        i = 0 if up else 1
        return pltpu.make_async_remote_copy(
            src_ref=src, dst_ref=dst, send_sem=halo_send.at[i], recv_sem=halo_recv.at[i],
            device_id=(dom + 1 if up else dom - 1, me), device_id_type=MESH)

    rows = jnp.where(kind < 3, kind + 1, kind + 2)
    peers = jnp.where(kind == 7, NG - 1, rows * 8 - 1 - (dom == 0).astype(I32))
    low = (has_low & jnp.logical_not(above_first)).astype(I32)
    pl.semaphore_wait(barrier, peers + low + has_high.astype(I32))

    @pl.when(has_high)
    def _():
        halo(True).start()

    @pl.when(kind == 7)
    def _():
        pl.semaphore_signal(late_z, inc=1, device_id=(dom + 1, me), device_id_type=MESH)

    @pl.when(has_low & jnp.logical_not(above_first))
    def _():
        halo(False).start()

    here = jnp.where(kind == 7, 8, y)

    def answer(d, c):
        q = (me + d) & (NG - 1)

        @pl.when(kind_of(dom, q) < kind)
        def _():
            pl.semaphore_signal(late.at[here], inc=1, device_id=(dom, q), device_id_type=MESH)

        return c

    lax.fori_loop(1, NG, answer, 0)

    tgt_copy.wait()
    tab_v[...] = routing(tgt_v, device)
    tab_copy = pltpu.make_async_copy(tab_v, tab_s, small_sem.at[2])
    tab_copy.start()

    left = iota((R, L), 1) < 64
    row64, col64 = iota((64, 64), 0), iota((64, 64), 1)
    woven = jnp.where(row64 == ((col64 & 31) << 1) + (col64 >> 5), 1.0, 0.0).astype(BF16)
    even = jnp.where(iota((R, L), 1) == iota((R, L), 0) * 2, 1.0, 0.0).astype(BF16)

    def spread_block(c, b):
        br = pltpu.roll(b, 64, 1)
        parts = jnp.concatenate(
            [jnp.concatenate([jnp.where(left, b, 0.0), jnp.where(left, 0.0, br)], axis=1),
             jnp.concatenate([jnp.where(left, br, 0.0), jnp.where(left, 0.0, b)], axis=1)], axis=0).astype(BF16)
        z = jnp.dot(woven, parts, preferred_element_type=F32).astype(BF16)
        w[c, 0:64, :] = z
        w[c, 64:128, 0:L] = z[:, L:]
        w[c, 64:128, L:2 * L] = z[:, :L]

    def prepare(e, c):
        b = pf[pl.ds(e, R, stride=E), :]
        spread_block(HALO + e, b)
        stacked = jnp.concatenate(
            [b, pltpu.roll(b, 63, 1), pltpu.roll(b, 64, 1), pltpu.roll(b, 127, 1)], axis=0).astype(BF16)
        ptx[e] = lax.dot_general(
            even, stacked, (((1,), (1,)), ((), ())), preferred_element_type=F32).astype(BF16)
        return c

    lax.fori_loop(0, E, prepare, 0, unroll=4)

    def unpack(k, c):
        for r in range(R):
            af[pl.ds(r * E, E), :] = a_v[k, :, r * L:(r + 1) * L].astype(F32)
        for e in range(E):
            a2[k * E + e] = af[pl.ds(e, R, stride=E), :].astype(BF16)
        return c

    for i in range(K):
        a_copies[i].wait()
    lax.fori_loop(0, K, unpack, 0)
    col_copy.wait()
    tab_copy.wait()

    @pl.when(above_first)
    def _():
        pl.semaphore_wait(late_z, 1)
        halo(False).start()

    @pl.when(has_low)
    def _():
        halo(True).wait_recv()

    @pl.when(has_high)
    def _():
        halo(False).wait_recv()

    def prepare_halo(i, c):
        at = jnp.where(i < HALO, i, i + E)
        spread_block(at, p2[at].astype(F32))
        return c

    lax.fori_loop(0, 2 * HALO, prepare_halo, 0, unroll=12)

    first_own = device * E

    def term(u):
        u = jnp.clip(u, 0, UNITS - 1)
        k, e = split(u)
        rel = col_s[k, e] - first_own
        at = jnp.where(rel < 0, rel + NG * E - (E - HALO), jnp.where(rel < E, rel + HALO, rel - NG * E + HALO + E))
        at = jnp.clip(at, 0, NP - 1)
        out = jnp.dot(a2[u], w[at], preferred_element_type=F32)
        one, two = out[:, :L], out[:, L:]
        right = jnp.concatenate(
            [jnp.where(left, one, 0.0), jnp.where(left, 0.0, one),
             jnp.where(left, two, 0.0), jnp.where(left, 0.0, two)], axis=0).astype(BF16)
        return jnp.dot(ptx[e], right, preferred_element_type=F32)

    def pay(q):
        return pltpu.make_async_remote_copy(
            src_ref=send_v.at[q], dst_ref=recv_ref.at[me], send_sem=pay_send, recv_sem=pay_recv,
            device_id=(dom, q), device_id_type=MESH)

    def lab(q):
        return pltpu.make_async_remote_copy(
            src_ref=lab_v.at[q], dst_ref=lab_ref.at[me], send_sem=lab_send, recv_sem=lab_recv,
            device_id=(dom, q), device_id_type=MESH)

    lane = iota((1, L), 1)

    def fill(q):
        for s in range(CAP):
            send_v[q, s * R:(s + 1) * R, :] = term(tab_s[s, q]).astype(BF16)
        lab_v[q] = jnp.where(lane == 0, tab_s[2, q], tab_s[3, q])

    def send(n, c):
        turn, pair = n >> 2, n & 3
        dx = (2 - turn) & 3
        dx = jnp.where(turn == 2, 3, jnp.where(turn == 3, 0, dx))
        pair = jnp.where(turn == 0, (pair + 1) & 3, pair)
        to_ys = []
        for j, far in enumerate(((y + 4 + pair) & 7, (y + 3 - pair) & 7)):
            i = pair * 2 + j
            by_kind = jnp.where(i < 3, i, jnp.where(i == 3, 7, jnp.where(i == 4, 3, 11 - i)))
            to_ys.append(jnp.where(turn >= 2, by_kind, far))
        peers = [(((x + dx) & 3) * 8 + to_y) * 2 + ((core + j) & 1) for to_y in to_ys for j in range(2)]
        for q in peers:
            fill(q)

        for to_y in to_ys:
            @pl.when((n < 4) & (jnp.where(to_y < 4, to_y, 10 - to_y) > kind))
            def _():
                pl.semaphore_wait(late.at[to_y], 8)

        for q in peers:
            @pl.when((q != me) & ((dom > 0) | (q > 0)))
            def _():
                lab(q).start()
                pay(q).start()
        return c

    lax.fori_loop(0, 16, send, 0)

    @pl.when((dom == 0) & (me > 0))
    def _():
        pl.semaphore_wait(late.at[8], 1)
        lab(0).start()
        pay(0).start()

    def at_home(i, acc):
        n = i * 8
        terms = []
        for j in range(8):
            pos = n + j
            terms.append(term(tab_s[4 + (pos >> 7), pos & 127]))
        for j in range(8):
            pos = n + j
            prev = jnp.maximum(pos - 1, 0)
            same = (tab_s[6 + (pos >> 7), pos & 127] == tab_s[6 + (prev >> 7), prev & 127]).astype(F32)
            acc = acc * same + terms[j]
            acc_v[pos] = acc
        return acc

    lax.fori_loop(0, UNITS // 8, at_home, jnp.zeros((R, L), F32))

    def fetch(t, c):
        home_v[t] = acc_v[jnp.clip(tab_s[8, t], 0, UNITS - 1)] * tab_s[9, t].astype(F32)
        return c

    lax.fori_loop(0, CB, fetch, 0, unroll=4)
    home_copy = pltpu.make_async_copy(home_v, home_ref, small_sem.at[3])
    home_copy.start()

    def all_pay():
        return pltpu.make_async_remote_copy(
            src_ref=send_v.at[pl.ds(0, NG - 1)], dst_ref=recv_ref.at[pl.ds(0, NG - 1)], send_sem=pay_send,
            recv_sem=pay_recv, device_id=(dom, me ^ 1), device_id_type=MESH)

    def all_lab():
        return pltpu.make_async_remote_copy(
            src_ref=lab_v.at[pl.ds(0, NG - 1)], dst_ref=lab_ref.at[pl.ds(0, NG - 1)], send_sem=lab_send,
            recv_sem=lab_recv, device_id=(dom, me ^ 1), device_id_type=MESH)

    @pl.when(has_high)
    def _():
        halo(True).wait_send()

    @pl.when(has_low)
    def _():
        halo(False).wait_send()

    home_copy.wait()
    all_lab().wait()
    all_pay().wait()


def collect(recv_ref, lab_ref, home_ref, out_ref, recv_v, lab_s, acc, acc_b, turned, out_v, rsem, lsem, hsem, osem):
    me = lax.axis_index("grp")
    lab_copy = pltpu.make_async_copy(lab_ref, lab_s, lsem)
    lab_copy.start()
    home_copy = pltpu.make_async_copy(home_ref, acc.at[pl.ds(0, CB)], hsem)
    home_copy.start()
    copies = [pltpu.make_async_copy(recv_ref.at[pl.ds(i * 16, 16)], recv_v.at[pl.ds(i * 16, 16)], rsem.at[i]) for i in range(4)]
    for c in copies:
        c.start()
    acc_b[...] = jnp.zeros_like(acc_b)
    lab_copy.wait()
    home_copy.wait()

    def add(d, c):
        for s, total in ((0, acc), (1, acc_b)):
            t = jnp.where(d == me, CB, jnp.clip(lab_s[d, 0, s], 0, CB))
            total[t] = total[t] + recv_v[d, s * R:(s + 1) * R, :].astype(F32)
        return c

    for i in range(4):
        copies[i].wait()
        lax.fori_loop(i * 16, i * 16 + 16, add, 0, unroll=16)

    outs = []
    for g in range(0, CB, 8):
        for t in range(g, g + 8):
            turned[pl.ds(t, R, stride=CB), :] = acc[t] + acc_b[t]
        for r in range(R):
            out_v[g:g + 8, r * L:(r + 1) * L] = turned[r * CB + g:r * CB + g + 8, :]
        outs.append(pltpu.make_async_copy(out_v.at[pl.ds(g, 8)], out_ref.at[pl.ds(g, 8)], osem.at[g // 8]))
        outs[-1].start()
    for c in outs:
        c.wait()


def on_device(a_blocks, p_blocks, columns, targets):
    hbm = pl.BlockSpec(memory_space=pl.ANY)
    dma = pltpu.SemaphoreType.DMA
    recv, labels, home = pl.pallas_call(
        exchange,
        out_shape=(
            jax.ShapeDtypeStruct((NG, CAP * R, L), BF16),
            jax.ShapeDtypeStruct((NG, 1, L), I32),
            jax.ShapeDtypeStruct((CB, R, L), F32),
        ),
        in_specs=[hbm] * 4,
        out_specs=(hbm, hbm, hbm),
        scratch_shapes=[
            pltpu.VMEM((K, E, 64 * 64), BF16),
            pltpu.VMEM((E, 64 * 64), BF16),
            pltpu.SMEM((K, E), I32),
            pltpu.VMEM((K, E), I32),
            pltpu.VMEM((16, L), I32),
            pltpu.SMEM((16, L), I32),
            pltpu.VMEM((R * E + E, L), F32),
            pltpu.VMEM((NP, R, L), BF16),
            pltpu.VMEM((NP, L, 2 * L), BF16),
            pltpu.VMEM((E, R, L), BF16),
            pltpu.VMEM((R * E + E, L), F32),
            pltpu.VMEM((UNITS, R, L), BF16),
            pltpu.VMEM((NG, CAP * R, L), BF16),
            pltpu.VMEM((NG, 1, L), I32),
            pltpu.VMEM((E * K, R, L), F32),
            pltpu.VMEM((CB, R, L), F32),
            dma((K,)), dma((2,)), dma((4,)), dma((2,)), dma((2,)), dma, dma, dma, dma,
            pltpu.SemaphoreType.REGULAR((9,)), pltpu.SemaphoreType.REGULAR,
        ],
        compiler_params=pltpu.CompilerParams(
            collective_id=0, has_side_effects=True, vmem_limit_bytes=62 * 1024 * 1024),
    )(a_blocks.transpose(1, 0, 2), p_blocks, columns.T, targets.T)
    return pl.pallas_call(
        collect,
        out_shape=jax.ShapeDtypeStruct((CB, 64 * 64), F32),
        in_specs=[hbm] * 3,
        out_specs=hbm,
        scratch_shapes=[
            pltpu.VMEM((NG, CAP * R, L), BF16),
            pltpu.SMEM((NG, 1, L), I32),
            pltpu.VMEM((CB + 1, R, L), F32),
            pltpu.VMEM((CB + 1, R, L), F32),
            pltpu.VMEM((R * CB + CB, L), F32),
            pltpu.VMEM((CB, 64 * 64), F32),
            dma((4,)), dma, dma, dma((4,)),
        ],
        compiler_params=pltpu.CompilerParams(vmem_limit_bytes=62 * 1024 * 1024),
    )(recv, labels, home)


def solution(mesh):
    spec = P(("dom", "grp"), None)
    return jax.shard_map(
        on_device, mesh=mesh, in_specs=(P(("dom", "grp"), None, None), spec, spec, spec), out_specs=spec,
        check_vma=False)
```
